128 devices in a mesh: ctx: 32 (over x, z, core), qh: 4 (over y).
Axes of the slice: x: 4, y: 4, z: 4, core: 2. Of those that a mesh axis runs over, the one named last changes fastest.
Arguments:
- queries: bfloat16 [16384, 1024], P('ctx', 'qh'), may hold values from -12 to 12
- keys: bfloat16 [32768, 128], P('ctx'), may hold values from -6 to 6
- values: bfloat16 [32768, 128], P('ctx'), may hold values from -6 to 6
- block_order: int32 [32], replicated, may hold values from 0 to 31, each once
Outputs:
- attended: bfloat16 [16384, 1024], P('ctx', 'qh')
The draws below stay inside these ranges and needn't reach their ends.
All inputs are finite; a program needn't handle non-finite values.
Results may differ from the reference program's by a relative error of at most 0.0065.
Values may be sent and summed in bfloat16 or wider, within the bound.
No kernel may reach another device: no remote copies, remote signals or barrier semaphores. Data moves between devices by JAX's collectives and lax.ppermute only.
A program may use at most 192 MiB of HBM per device.

```python
import math
import jax
import jax.numpy as jnp
from jax import lax

HD = 128
HEADS = 8
KV_DEV = 1024
QB = 512
CTX = 32768
QTOK = 16384
N_CTX = 32


def draw_queries(key, part):
    key = jax.random.fold_in(key, 11)
    base = 3.0 * jnp.clip(jax.random.normal(key, (QTOK, HEADS * HD), jnp.float32), -4.0, 4.0)
    return base.astype(jnp.bfloat16)


def draw_keys(key, part):
    key = jax.random.fold_in(key, 23)
    base = jnp.clip(jax.random.normal(key, (CTX, HD), jnp.float32), -6.0, 6.0)
    return base.astype(jnp.bfloat16)


def block_scale(own_key, extent, shards, low, largest):
    loudness = 1.0
    for axis_at, parts in shards:
        draws = jax.random.uniform(jax.random.fold_in(jax.random.fold_in(own_key, 6), axis_at), (parts,), jnp.float32, low / len(shards), largest / len(shards))
        loudness = loudness * jnp.repeat(jnp.exp(draws), extent[axis_at] // parts).reshape((-1,) + (1,) * (len(extent) - 1 - axis_at))
    return loudness


def centred(stream_key, shape, width, limit, split=(), held_as=jnp.bfloat16):
    array = width * jax.random.normal(stream_key, shape, jnp.float32)
    if split:
        array = array * block_scale(stream_key, shape, split, -0.22, 0.18)
    return jnp.clip(array, -limit, limit).astype(held_as)


def setup_inputs(seed: int = 0) -> dict:
    arg_keys = jax.random.split(jax.random.key(seed), 5)
    queries = draw_queries(jax.random.fold_in(arg_keys[4], 71), 0)
    keys = draw_keys(jax.random.fold_in(arg_keys[4], 71), 0)
    values = centred(arg_keys[2], (CTX, HD), 1.0, 6.0, ((0, 32),))
    block_order = jax.random.permutation(arg_keys[3], N_CTX).astype(jnp.int32)
    return dict(queries=queries, keys=keys, values=values, block_order=block_order)


def block_terms(query_part, key_block, value_block, query_pos, key_start):
    inv_root = 1.0 / math.sqrt(HD)
    scores = jnp.einsum('rhd,kd->rhk', query_part, key_block.astype(jnp.float32)) * inv_root
    key_pos = key_start + jnp.arange(key_block.shape[0], dtype=jnp.int32)
    visible = key_pos[None, None, :] <= query_pos[:, None, None]
    maxima = lax.optimization_barrier(jnp.max(jnp.where(visible, scores, -1e+30), axis=-1))
    probability = jnp.where(visible, jnp.exp(scores - maxima[..., None]), 0.0).astype(jnp.bfloat16)
    prob_float = probability.astype(jnp.float32)
    totals = lax.optimization_barrier(jnp.sum(prob_float, axis=-1))
    output = jnp.einsum('rhk,kd->rhd', prob_float, value_block.astype(jnp.float32))
    return (maxima, totals, output)

def reference(queries, keys, values, block_order):
    row_count = queries.shape[0]
    block_rows = math.gcd(1024, row_count)
    row_ids = jnp.arange(row_count, dtype=jnp.int32)
    query_pos = CTX - QTOK + block_order[row_ids // QB] * QB + row_ids % QB
    query_blocks = queries.reshape(row_count // block_rows, block_rows, HEADS, HD)
    pos_blocks = query_pos.reshape(row_count // block_rows, block_rows)
    key_blocks = keys.reshape(N_CTX, KV_DEV, HD)
    value_blocks = values.reshape(N_CTX, KV_DEV, HD)

    def one_block(operands):
        query_block, pos_block = operands
        query_float = query_block.astype(jnp.float32)

        def advance(running, entry):
            best, summed, gathered = running
            key_block, value_block, block_index = entry
            maxima, totals, output = block_terms(query_float, key_block, value_block, pos_block, block_index * KV_DEV)
            newest = jnp.maximum(best, maxima)
            old_weight = jnp.exp(best - newest)
            new_weight = jnp.exp(maxima - newest)
            return ((newest, summed * old_weight + totals * new_weight, gathered * old_weight[..., None] + output * new_weight[..., None]), None)
        start_state = (jnp.full((block_rows, HEADS), -1e+30, jnp.float32), jnp.zeros((block_rows, HEADS), jnp.float32), jnp.zeros((block_rows, HEADS, HD), jnp.float32))
        final_state, unused = lax.scan(advance, start_state, (key_blocks, value_blocks, jnp.arange(N_CTX, dtype=jnp.int32)))
        best, summed, gathered = final_state
        return (gathered / summed[..., None]).astype(jnp.bfloat16)
    attended = lax.map(one_block, (query_blocks, pos_blocks))
    return attended.reshape(row_count, HEADS * HD)
```

```python
import math

import jax
import jax.numpy as jnp
from jax import lax
from jax.experimental import pallas as pl
from jax.experimental.pallas import tpu as pltpu
from jax.sharding import Mesh, PartitionSpec as P

HD = 128
KV_DEV = 1024
QB = 512
HEADS_DEV = 2
QROWS = QB * HEADS_DEV
SUMS = 16
SAMPLE = 128
PART = 512
FIRST_BLOCK = 16
SCALE = 1.4426950408889634 / math.sqrt(HD)
LOW = -1e30
SAFE = 2.0**100
NZ = 4
HERE = ((0, 0), (0, 1), (1, 0), (3, 0))
LATER = ((1, 1), (3, 1), (2, 0), (2, 1))
STATS = 16
NT = (((1,), (1,)), ((), ()))


def ring(size, step):
    return [(i, (i + step) % size) for i in range(size)]


def swap_core(value):
    return lax.ppermute(value, "core", [(0, 1), (1, 0)])


def scores(keys, q):
    return lax.dot_general(keys, q, NT, preferred_element_type=jnp.float32)


def visible_keys(order, block, first, count):
    k_pos = block * KV_DEV + first + lax.broadcasted_iota(jnp.int32, (count, QB), 0)
    q_pos = FIRST_BLOCK * KV_DEV + order * QB + lax.broadcasted_iota(jnp.int32, (count, QB), 1)
    return k_pos <= q_pos


def q_head(q_s, qi, head):
    return q_s[qi, :, head * HD : (head + 1) * HD]


def keys_of(kv_s, kj):
    return kv_s[kj, :KV_DEV, :]


def values_product(kv_s, kj, p, first=0):
    count = p.shape[0]
    starts = [KV_DEV + first + i for i in range(0, count, HD)]
    across = jnp.concatenate([kv_s[kj, pl.ds(i, HD), :] for i in starts], axis=1)
    tall = jnp.concatenate([across, jnp.ones((SUMS, count), jnp.bfloat16)], axis=0)
    return jnp.dot(tall, p, preferred_element_type=jnp.float32)


def stat_row(head, piece, half):
    return (head * 3 + piece) * 2 + half


def probabilities(s, ref_point):
    return jnp.exp2(s * SCALE - ref_point)


def masked_step(q_s, kv_s, m_s, acc_s, qi, kj, order, block, first):
    visible = visible_keys(order, block, first, QB)
    for head in range(HEADS_DEV):
        s = scores(kv_s[kj, pl.ds(first, QB), :], q_head(q_s, qi, head))
        p = probabilities(s, m_s[qi, head, :1, :])
        p = jnp.where(visible, p, 0.0).astype(jnp.bfloat16)
        acc_s[qi, head] += values_product(kv_s, kj, p, first)


def running_step(q_s, kv_s, m_s, acc_s, qi, kj, order, block, first):
    visible = visible_keys(order, block, first, PART)
    for head in range(HEADS_DEV):
        s = scores(kv_s[kj, pl.ds(first, PART), :], q_head(q_s, qi, head))
        s = jnp.where(visible, s * SCALE, LOW)
        m_old = m_s[qi, head]
        m_new = jnp.maximum(m_old, jnp.max(s, axis=0, keepdims=True))
        p = jnp.where(visible, jnp.exp2(s - m_new[:1]), 0.0).astype(jnp.bfloat16)
        m_s[qi, head] = m_new
        acc_s[qi, head] = acc_s[qi, head] * jnp.exp2(m_old - m_new)[:1] + values_product(
            kv_s, kj, p, first
        )


def attend_kernel(z_steps, kv_steps, pairs, resumed, final, order_in, *refs):
    nq, nkv = len(z_steps), len(kv_steps)
    now = 1 + max(kj for _, kj in pairs)
    refs = list(refs)
    q_in = [refs.pop(0) for _ in range(nq)]
    kv_in = [refs.pop(0) for _ in range(nkv)]
    state_in = {i: (refs.pop(0), refs.pop(0)) for i in resumed}
    if final:
        outs = [refs.pop(0) for _ in range(nq)]
    else:
        state_out = [(refs.pop(0), refs.pop(0)) for _ in range(nq)]
    acc_s, m_s, q_s, kv_s, s_s, p_s, order_ref, list_q, list_k, edge_s, block_s = refs[:11]
    order_sem, kv_sem = refs[11:]
    x = lax.axis_index("x")
    z = lax.axis_index("z")
    core = lax.axis_index("core")

    def kv_copy(j, half, source=1):
        rows = pl.ds(half * KV_DEV, KV_DEV)
        return pltpu.make_async_copy(
            kv_in[source].at[rows, :], kv_s.at[j, rows, :], kv_sem.at[j, half]
        )

    order_copy = pltpu.make_async_copy(order_in, order_ref, order_sem)
    kv_copies = [kv_copy(j, half, j) for j in range(nkv) for half in range(2)]
    for copy in [order_copy, *kv_copies[2 : 2 * now]]:
        copy.start()
    for i in range(nq):
        q_s[i] = q_in[i][...]
    kv_s[0] = kv_in[0][...]
    acc_s[...] = jnp.zeros(acc_s.shape, jnp.float32)
    p_s[...] = jnp.zeros(p_s.shape, jnp.bfloat16)
    for i in range(nq):
        if i in resumed:
            m_s[i] = state_in[i][1][...]
            continue
        for head in range(HEADS_DEV):
            s = scores(kv_s[0, :SAMPLE, :], q_head(q_s, i, head))
            top = jnp.max(s, axis=0, keepdims=True) * SCALE
            m_s[i, head] = jnp.broadcast_to(top, (8, QB))
    order_copy.wait()

    orders = [order_ref[x * 8 + lax.rem(z + step, 4) * 2 + core] for step in z_steps]
    blocks = [
        lax.rem(x + x_step, 4) * 8 + z * 2 + lax.rem(core + core_step, 2)
        for x_step, core_step in kv_steps
    ]
    for j, block in enumerate(blocks):
        block_s[j] = block
    count = edges = jnp.int32(0)
    for qi, kj in pairs:
        last = FIRST_BLOCK + orders[qi] // 2
        list_q[count] = qi
        list_k[count] = kj
        count += (blocks[kj] < last).astype(jnp.int32)
        for first in (0, QB):
            for column, value in enumerate((qi, kj, orders[qi], blocks[kj], first)):
                edge_s[edges, column] = value
            seen = (blocks[kj] == last) & ((first == 0) | (lax.rem(orders[qi], 2) == 1))
            edges += seen.astype(jnp.int32)

    def wait_upto(done, needed):
        def wait_one(j, carry):
            for half in range(2):
                kv_copy(j, half).wait()
            return carry

        lax.fori_loop(done, needed + 1, wait_one, 0)
        return jnp.maximum(done, needed + 1)

    parts = range(0, KV_DEV, PART)

    def pair(t, carry):
        q_old, k_old, here = carry
        qi, kj = list_q[t], list_k[t]
        after = jnp.minimum(t + 1, count - 1)
        q_next, k_next = list_q[after], list_k[after]
        here = wait_upto(here, k_next)
        s = [s_s[i : i + PART, :] for i in parts]
        p_old = [p_s[i : i + PART, :] for i in parts]
        for head in range(HEADS_DEV):
            if head + 1 < HEADS_DEV:
                q_then, k_then, head_then = qi, kj, head + 1
            else:
                q_then, k_then, head_then = q_next, k_next, 0
            if head > 0:
                q_old, k_old = qi, kj
            head_old = (head - 1) % HEADS_DEV
            ref_point = m_s[qi, head, :1, :]
            s_next, p_new, total = [], [], acc_s[q_old, head_old]
            for n, i in enumerate(parts):
                s_next.append(
                    scores(kv_s[k_then, i : i + PART, :], q_head(q_s, q_then, head_then))
                )
                p_new.append(probabilities(s[n], ref_point).astype(jnp.bfloat16))
                total = total + values_product(kv_s, k_old, p_old[n], i)
            acc_s[q_old, head_old] = total
            s, p_old = s_next, p_new
        for n, i in enumerate(parts):
            s_s[i : i + PART, :] = s[n]
            p_s[i : i + PART, :] = p_old[n]
        return qi, kj, here

    here = wait_upto(jnp.int32(1), list_k[0])
    s_s[...] = scores(keys_of(kv_s, list_k[0]), q_head(q_s, list_q[0], 0))
    q_last, k_last, here = lax.fori_loop(0, count, pair, (list_q[0], list_k[0], here))
    wait_upto(here, jnp.int32(now - 1))

    def edge(t, carry):
        qi, kj, order, block = [edge_s[t, column] for column in range(4)]
        first = pl.multiple_of(edge_s[t, 4], QB)
        masked_step(q_s, kv_s, m_s, acc_s, qi, kj, order, block, first)
        return carry

    lax.fori_loop(0, edges, edge, 0)
    q_last = 0 if nq == 1 else q_last
    acc_s[q_last, HEADS_DEV - 1] += values_product(kv_s, k_last, p_s[...])
    if not final:
        for i in range(nq):
            state_out[i][0][...] = acc_s[i]
            state_out[i][1][...] = m_s[i]
        return
    for i in resumed:
        acc_s[i] += state_in[i][0][...]

    row = lax.broadcasted_iota(jnp.int32, (STATS, HEADS_DEV * HD), 0)

    def finish(i):
        logs = jnp.zeros((STATS, HEADS_DEV * HD), jnp.float32)
        for head in range(HEADS_DEV):
            total = acc_s[i, head, HD : HD + 1, :]
            outs[i][:QB, head * HD : (head + 1) * HD] = (
                (acc_s[i, head, :HD, :] * (1.0 / total)).T.astype(jnp.bfloat16)
            )
            rest = m_s[i, head, :1, :] + jnp.log2(total)
            for piece in range(3):
                part = rest.astype(jnp.bfloat16).astype(jnp.float32)
                for half in range(2):
                    columns = part[:, half * HEADS_DEV * HD : (half + 1) * HEADS_DEV * HD]
                    logs = jnp.where(row == stat_row(head, piece, half), columns, logs)
                rest = rest - part
        outs[i][QB:, :] = logs.astype(jnp.bfloat16)

    def redo(qi, order):
        m_s[qi] = jnp.full(m_s.shape[1:], LOW, jnp.float32)
        acc_s[qi] = jnp.zeros(acc_s.shape[1:], jnp.float32)

        def step(t, carry):
            kj = t // (KV_DEV // PART)
            first = pl.multiple_of(lax.rem(t, KV_DEV // PART) * PART, PART)
            block = block_s[kj]

            @pl.when(block <= FIRST_BLOCK + order // 2)
            def _():
                running_step(q_s, kv_s, m_s, acc_s, qi, kj, order, block, first)

            return carry

        lax.fori_loop(0, nkv * (KV_DEV // PART), step, 0)

    for i in range(nq):
        finish(i)
    totals = acc_s[:, :, HD : HD + 8, :]
    bad = jnp.max(jnp.where((totals > 1.0 / SAFE) & (totals < SAFE), 0.0, 1.0))

    @pl.when(bad > 0.0)
    def _():
        for copy in kv_copies[2 * now :]:
            copy.start()
        for copy in kv_copies[2 * now :]:
            copy.wait()
        for i in range(nq):
            redo(i, orders[i])
            finish(i)


def attend(block_order, queries, z_steps, blocks, kv_steps, pairs, states=None, final=True):
    states = states or {}
    nq, nkv = len(queries), len(kv_steps)
    any_spec = pl.BlockSpec(memory_space=pl.ANY)
    vmem_spec = pl.BlockSpec(memory_space=pltpu.VMEM)
    acc_shape, m_shape = (HEADS_DEV, HD + SUMS, QB), (HEADS_DEV, 8, QB)
    if final:
        outs = [jax.ShapeDtypeStruct((QB + STATS, HEADS_DEV * HD), jnp.bfloat16)] * nq
    else:
        outs = [jax.ShapeDtypeStruct(shape, jnp.float32) for shape in (acc_shape, m_shape)] * nq
    results = pl.pallas_call(
        lambda *refs: attend_kernel(z_steps, kv_steps, pairs, sorted(states), final, *refs),
        out_shape=outs,
        in_specs=[any_spec]
        + [vmem_spec] * (nq + 1)
        + [any_spec] * (nkv - 1)
        + [vmem_spec] * (2 * len(states)),
        out_specs=[vmem_spec] * len(outs),
        scratch_shapes=[
            pltpu.VMEM((nq, *acc_shape), jnp.float32),
            pltpu.VMEM((nq, *m_shape), jnp.float32),
            pltpu.VMEM((nq, QB, HEADS_DEV * HD), jnp.bfloat16),
            pltpu.VMEM((nkv, 2 * KV_DEV, HD), jnp.bfloat16),
            pltpu.VMEM((KV_DEV, QB), jnp.float32),
            pltpu.VMEM((KV_DEV, QB), jnp.bfloat16),
            pltpu.SMEM(block_order.shape, jnp.int32),
            pltpu.SMEM((len(pairs) + 1,), jnp.int32),
            pltpu.SMEM((len(pairs) + 1,), jnp.int32),
            pltpu.SMEM((2 * len(pairs) + 1, 5), jnp.int32),
            pltpu.SMEM((nkv,), jnp.int32),
            pltpu.SemaphoreType.DMA,
            pltpu.SemaphoreType.DMA((nkv, 2)),
        ],
        compiler_params=pltpu.CompilerParams(vmem_limit_bytes=28 * 1024 * 1024),
        cost_estimate=pl.CostEstimate(
            flops=4 * len(pairs) * QROWS * KV_DEV * HD,
            bytes_accessed=nq * QROWS * HD * 4 + nkv * KV_DEV * HD * 4,
            transcendentals=len(pairs) * QROWS * KV_DEV,
        ),
        name="attend",
    )(
        block_order,
        *queries,
        *[blocks[step] for step in kv_steps],
        *[array for i in sorted(states) for array in states[i]],
    )
    return results if final else [tuple(results[2 * i : 2 * i + 2]) for i in range(nq)]


def pack(keys, values):
    pieces = values.reshape(KV_DEV // HD, HD, HD).swapaxes(1, 2).reshape(KV_DEV, HD)
    return jnp.concatenate([keys, pieces], axis=0)


def combine_kernel(*refs):
    parts, result = refs[:NZ], refs[NZ]
    stats = [part[QB:, :].astype(jnp.float32) for part in parts]
    for head in range(HEADS_DEV):
        logs = []
        for stat in stats:
            halves = []
            for half in range(2):
                rows = [stat_row(head, piece, half) for piece in range(3)]
                halves.append(sum(stat[r : r + 1, :] for r in rows))
            logs.append(jnp.concatenate(halves, axis=1))
        top = logs[0]
        for log in logs[1:]:
            top = jnp.maximum(top, log)
        weights = [jnp.exp2(log - top) for log in logs]
        share = 1.0 / sum(weights)
        columns = slice(head * HD, (head + 1) * HD)
        gathered = jnp.zeros((QB, HD), jnp.float32)
        for weight, part in zip(weights, parts):
            across = jnp.broadcast_to(weight * share, (HD, QB)).T
            gathered = gathered + across * part[:QB, columns].astype(jnp.float32)
        result[:, columns] = gathered.astype(jnp.bfloat16)


def combine(parts):
    vmem_spec = pl.BlockSpec(memory_space=pltpu.VMEM)
    return pl.pallas_call(
        combine_kernel,
        out_shape=jax.ShapeDtypeStruct((QB, HEADS_DEV * HD), jnp.bfloat16),
        in_specs=[vmem_spec] * NZ,
        out_specs=vmem_spec,
        compiler_params=pltpu.CompilerParams(vmem_limit_bytes=32 * 1024 * 1024),
        cost_estimate=pl.CostEstimate(
            flops=8 * NZ * QROWS * HD,
            bytes_accessed=(NZ + 1) * QROWS * HD * 2,
            transcendentals=NZ * QROWS,
        ),
        name="combine",
    )(*parts)


def every(queries, keys):
    return tuple((qi, kj) for qi in queries for kj in keys)


def body(queries, keys, values, block_order):
    def key_block(step):
        return lax.ppermute(own, "x", ring(4, -step))

    def query_block(value, step):
        return lax.ppermute(value, "z", ring(4, -step))

    def give_back(part, step):
        return lax.ppermute(part, "z", ring(4, step))

    own = pack(keys, values)
    blocks = {(0, 0): own, (1, 0): key_block(1), (3, 0): key_block(3), (0, 1): swap_core(own)}
    back, ahead = query_block(queries, 3), query_block(queries, 1)
    far, back, ahead = lax.optimization_barrier((queries, back, ahead))
    far = query_block(far, 2)
    near = blocks[1, 0], blocks[3, 0]
    own, back, ahead, near = lax.optimization_barrier((own, back, ahead, near))
    blocks[1, 0], blocks[3, 0] = near
    blocks[2, 0] = key_block(2)
    for step in (1, 3):
        blocks[step, 1] = swap_core(blocks[step, 0])
    *states, own_state = attend(
        block_order,
        [back, ahead, queries],
        (3, 1, 0),
        blocks,
        HERE,
        every((0, 1), range(4)) + every((2,), range(3)),
        final=False,
    )
    states, far, blocks[2, 0] = lax.optimization_barrier((states, far, blocks[2, 0]))
    blocks[2, 1] = swap_core(blocks[2, 0])
    to_back, to_ahead = attend(
        block_order,
        [back, ahead],
        (3, 1),
        blocks,
        LATER + HERE,
        every((0, 1), range(4)),
        dict(enumerate(states)),
    )
    to_back, to_ahead, far = lax.optimization_barrier((to_back, to_ahead, far))
    here = [give_back(to_back, 3), give_back(to_ahead, 1)]
    (to_far,) = attend(block_order, [far], (2,), blocks, HERE + LATER, every((0,), range(8)))
    to_far, queries, here = lax.optimization_barrier((to_far, queries, here))
    here.append(give_back(to_far, 2))
    last = LATER + HERE[::-1]
    (own_part,) = attend(
        block_order, [queries], (0,), blocks, last, every((0,), range(5)), {0: own_state}
    )
    return combine([own_part, *here])


def solution(mesh):
    split = Mesh(mesh.devices.reshape(4, 4, 2, 4), ("x", "z", "core", "qh"))
    ctx = ("x", "z", "core")
    in_specs = (P(ctx, "qh"), P(ctx, None), P(ctx, None), P())
    out_specs = P(ctx, "qh")
    return jax.shard_map(body, mesh=split, in_specs=in_specs, out_specs=out_specs, check_vma=False)
```

```python
import math

import jax
import jax.numpy as jnp
from jax import lax
from jax.experimental import pallas as pl
from jax.experimental.pallas import tpu as pltpu
from jax.sharding import Mesh, PartitionSpec as P

HD = 128
KV_DEV = 1024
QB = 512
HEADS_DEV = 2
QROWS = QB * HEADS_DEV
SUMS = 16
SAMPLE = 128
PART = 512
FIRST_BLOCK = 16
SCALE = 1.4426950408889634 / math.sqrt(HD)
LOW = -1e30
SAFE = 2.0**100
NZ = 4
HERE = ((0, 0), (0, 1), (1, 0), (3, 0))
LATER = ((1, 1), (3, 1), (2, 0), (2, 1))
FIRST = (3, 1)
EARLY_PAIRS = 10
STATS = 16
NT = (((1,), (1,)), ((), ()))


def ring(size, step):
    return [(i, (i + step) % size) for i in range(size)]


def swap_core(value):
    return lax.ppermute(value, "core", [(0, 1), (1, 0)])


def scores(keys, q):
    return lax.dot_general(keys, q, NT, preferred_element_type=jnp.float32)


def visible_keys(order, block, first, count):
    k_pos = block * KV_DEV + first + lax.broadcasted_iota(jnp.int32, (count, QB), 0)
    q_pos = FIRST_BLOCK * KV_DEV + order * QB + lax.broadcasted_iota(jnp.int32, (count, QB), 1)
    return k_pos <= q_pos


def q_head(q_s, qi, head):
    return q_s[qi, :, head * HD : (head + 1) * HD]


def keys_of(kv_s, kj):
    return kv_s[kj, :KV_DEV, :]


def values_product(kv_s, kj, p, first=0):
    count = p.shape[0]
    starts = [KV_DEV + first + i for i in range(0, count, HD)]
    across = jnp.concatenate([kv_s[kj, pl.ds(i, HD), :] for i in starts], axis=1)
    tall = jnp.concatenate([across, jnp.ones((SUMS, count), jnp.bfloat16)], axis=0)
    return jnp.dot(tall, p, preferred_element_type=jnp.float32)


def stat_row(head, piece, half):
    return (head * 3 + piece) * 2 + half


def probabilities(s, ref_point):
    return jnp.exp2(s * SCALE - ref_point)


def masked_step(q_s, kv_s, m_s, acc_s, qi, kj, order, block, first):
    visible = visible_keys(order, block, first, QB)
    for head in range(HEADS_DEV):
        s = scores(kv_s[kj, pl.ds(first, QB), :], q_head(q_s, qi, head))
        p = probabilities(s, m_s[qi, head, :1, :])
        p = jnp.where(visible, p, 0.0).astype(jnp.bfloat16)
        acc_s[qi, head] += values_product(kv_s, kj, p, first)


def running_step(q_s, kv_s, m_s, acc_s, qi, kj, order, block, first):
    visible = visible_keys(order, block, first, PART)
    for head in range(HEADS_DEV):
        s = scores(kv_s[kj, pl.ds(first, PART), :], q_head(q_s, qi, head))
        s = jnp.where(visible, s * SCALE, LOW)
        m_old = m_s[qi, head]
        m_new = jnp.maximum(m_old, jnp.max(s, axis=0, keepdims=True))
        p = jnp.where(visible, jnp.exp2(s - m_new[:1]), 0.0).astype(jnp.bfloat16)
        m_s[qi, head] = m_new
        acc_s[qi, head] = acc_s[qi, head] * jnp.exp2(m_old - m_new)[:1] + values_product(
            kv_s, kj, p, first
        )


def attend_kernel(z_steps, kv_steps, pairs, resumed, final, own_early, order_in, *refs):
    nq, nkv = len(z_steps), len(kv_steps)
    now = 1 + max(kj for _, kj in pairs)
    refs = list(refs)
    q_in = [refs.pop(0) for _ in range(nq)]
    kv_in = [refs.pop(0) for _ in range(nkv)]
    state_in = {i: (refs.pop(0), refs.pop(0)) for i in resumed}
    if final:
        outs = [refs.pop(0) for _ in range(nq)]
    else:
        state_out = [(refs.pop(0), refs.pop(0)) for _ in range(nq)]
    acc_s, m_s, q_s, kv_s, s_s, p_s, order_ref, list_q, list_k, edge_s, block_s = refs[:11]
    order_sem, kv_sem = refs[11:]
    x = lax.axis_index("x")
    z = lax.axis_index("z")
    core = lax.axis_index("core")

    def kv_copy(j, half, source=1):
        rows = pl.ds(half * KV_DEV, KV_DEV)
        return pltpu.make_async_copy(
            kv_in[source].at[rows, :], kv_s.at[j, rows, :], kv_sem.at[j, half]
        )

    order_copy = pltpu.make_async_copy(order_in, order_ref, order_sem)
    kv_copies = [kv_copy(j, half, j) for j in range(nkv) for half in range(2)]
    for copy in [order_copy, *kv_copies[2 : 2 * now]]:
        copy.start()
    for i in range(nq):
        q_s[i] = q_in[i][...]
    kv_s[0] = kv_in[0][...]
    acc_s[...] = jnp.zeros(acc_s.shape, jnp.float32)
    p_s[...] = jnp.zeros(p_s.shape, jnp.bfloat16)
    for i in range(nq):
        if i in resumed:
            m_s[i] = state_in[i][1][...]
            continue
        for head in range(HEADS_DEV):
            s = scores(kv_s[0, :SAMPLE, :], q_head(q_s, i, head))
            top = jnp.max(s, axis=0, keepdims=True) * SCALE
            m_s[i, head] = jnp.broadcast_to(top, (8, QB))
    order_copy.wait()

    def order_at(step):
        return order_ref[x * 8 + lax.rem(z + step, 4) * 2 + core]

    def block_at(step):
        return lax.rem(x + step[0], 4) * 8 + z * 2 + lax.rem(core + step[1], 2)

    def reaches(order, block):
        return block <= FIRST_BLOCK + order // 2

    orders = [order_at(step) for step in z_steps]
    blocks = [block_at(step) for step in kv_steps]
    taken = {}
    if own_early is not None:
        load = jnp.int32(0)
        for z_step in FIRST:
            for step in HERE:
                load += reaches(order_at(z_step), block_at(step)).astype(jnp.int32)
        for step in HERE:
            early = reaches(order_at(0), block_at(step)) & (load < EARLY_PAIRS)
            load += early.astype(jnp.int32)
            taken[step] = early if own_early else jnp.logical_not(early)
    for j, block in enumerate(blocks):
        block_s[j] = block
    count = edges = jnp.int32(0)
    for qi, kj in pairs:
        last = FIRST_BLOCK + orders[qi] // 2
        list_q[count] = qi
        list_k[count] = kj
        mine = taken.get(kv_steps[kj], True) if z_steps[qi] == 0 else True
        count += ((blocks[kj] < last) & mine).astype(jnp.int32)
        for first in (0, QB):
            for column, value in enumerate((qi, kj, orders[qi], blocks[kj], first)):
                edge_s[edges, column] = value
            seen = (blocks[kj] == last) & mine
            if first > 0:
                seen = seen & (lax.rem(orders[qi], 2) == 1)
            edges += seen.astype(jnp.int32)

    def wait_upto(done, needed):
        def wait_one(j, carry):
            for half in range(2):
                kv_copy(j, half).wait()
            return carry

        lax.fori_loop(done, needed + 1, wait_one, 0)
        return jnp.maximum(done, needed + 1)

    parts = range(0, KV_DEV, PART)

    def pair(t, carry):
        q_old, k_old, here = carry
        qi, kj = list_q[t], list_k[t]
        after = jnp.minimum(t + 1, count - 1)
        q_next, k_next = list_q[after], list_k[after]
        here = wait_upto(here, k_next)
        s = [s_s[i : i + PART, :] for i in parts]
        p_old = [p_s[i : i + PART, :] for i in parts]
        for head in range(HEADS_DEV):
            if head + 1 < HEADS_DEV:
                q_then, k_then, head_then = qi, kj, head + 1
            else:
                q_then, k_then, head_then = q_next, k_next, 0
            if head > 0:
                q_old, k_old = qi, kj
            head_old = (head - 1) % HEADS_DEV
            ref_point = m_s[qi, head, :1, :]
            s_next, p_new, total = [], [], acc_s[q_old, head_old]
            for n, i in enumerate(parts):
                s_next.append(
                    scores(kv_s[k_then, i : i + PART, :], q_head(q_s, q_then, head_then))
                )
                p_new.append(probabilities(s[n], ref_point).astype(jnp.bfloat16))
                total = total + values_product(kv_s, k_old, p_old[n], i)
            acc_s[q_old, head_old] = total
            s, p_old = s_next, p_new
        for n, i in enumerate(parts):
            s_s[i : i + PART, :] = s[n]
            p_s[i : i + PART, :] = p_old[n]
        return qi, kj, here

    here = wait_upto(jnp.int32(1), list_k[0])
    s_s[...] = scores(keys_of(kv_s, list_k[0]), q_head(q_s, list_q[0], 0))
    q_last, k_last, here = lax.fori_loop(0, count, pair, (list_q[0], list_k[0], here))
    wait_upto(here, jnp.int32(now - 1))

    def edge(t, carry):
        qi, kj, order, block = [edge_s[t, column] for column in range(4)]
        first = pl.multiple_of(edge_s[t, 4], QB)
        masked_step(q_s, kv_s, m_s, acc_s, qi, kj, order, block, first)
        return carry

    lax.fori_loop(0, edges, edge, 0)
    q_last = 0 if nq == 1 else q_last
    acc_s[q_last, HEADS_DEV - 1] += values_product(kv_s, k_last, p_s[...])
    if not final:
        for i in range(nq):
            state_out[i][0][...] = acc_s[i]
            state_out[i][1][...] = m_s[i]
        return
    for i in resumed:
        acc_s[i] += state_in[i][0][...]

    row = lax.broadcasted_iota(jnp.int32, (STATS, HEADS_DEV * HD), 0)

    def finish(i):
        logs = jnp.zeros((STATS, HEADS_DEV * HD), jnp.float32)
        for head in range(HEADS_DEV):
            total = acc_s[i, head, HD : HD + 1, :]
            outs[i][:QB, head * HD : (head + 1) * HD] = (
                (acc_s[i, head, :HD, :] * (1.0 / total)).T.astype(jnp.bfloat16)
            )
            rest = m_s[i, head, :1, :] + jnp.log2(total)
            for piece in range(3):
                part = rest.astype(jnp.bfloat16).astype(jnp.float32)
                for half in range(2):
                    columns = part[:, half * HEADS_DEV * HD : (half + 1) * HEADS_DEV * HD]
                    logs = jnp.where(row == stat_row(head, piece, half), columns, logs)
                rest = rest - part
        outs[i][QB:, :] = logs.astype(jnp.bfloat16)

    def redo(qi, order):
        m_s[qi] = jnp.full(m_s.shape[1:], LOW, jnp.float32)
        acc_s[qi] = jnp.zeros(acc_s.shape[1:], jnp.float32)

        def step(t, carry):
            kj = t // (KV_DEV // PART)
            first = pl.multiple_of(lax.rem(t, KV_DEV // PART) * PART, PART)
            block = block_s[kj]

            @pl.when(block <= FIRST_BLOCK + order // 2)
            def _():
                running_step(q_s, kv_s, m_s, acc_s, qi, kj, order, block, first)

            return carry

        lax.fori_loop(0, nkv * (KV_DEV // PART), step, 0)

    for i in range(nq):
        finish(i)
    totals = acc_s[:, :, HD : HD + 8, :]
    bad = jnp.max(jnp.where((totals > 1.0 / SAFE) & (totals < SAFE), 0.0, 1.0))

    @pl.when(bad > 0.0)
    def _():
        for copy in kv_copies[2 * now :]:
            copy.start()
        for copy in kv_copies[2 * now :]:
            copy.wait()
        for i in range(nq):
            redo(i, orders[i])
            finish(i)


def attend(
    block_order,
    queries,
    z_steps,
    blocks,
    kv_steps,
    pairs,
    states=None,
    final=True,
    own_early=None,
):
    states = states or {}
    nq, nkv = len(queries), len(kv_steps)
    any_spec = pl.BlockSpec(memory_space=pl.ANY)
    vmem_spec = pl.BlockSpec(memory_space=pltpu.VMEM)
    acc_shape, m_shape = (HEADS_DEV, HD + SUMS, QB), (HEADS_DEV, 8, QB)
    if final:
        outs = [jax.ShapeDtypeStruct((QB + STATS, HEADS_DEV * HD), jnp.bfloat16)] * nq
    else:
        outs = [jax.ShapeDtypeStruct(shape, jnp.float32) for shape in (acc_shape, m_shape)] * nq
    results = pl.pallas_call(
        lambda *refs: attend_kernel(
            z_steps, kv_steps, pairs, sorted(states), final, own_early, *refs
        ),
        out_shape=outs,
        in_specs=[any_spec]
        + [vmem_spec] * (nq + 1)
        + [any_spec] * (nkv - 1)
        + [vmem_spec] * (2 * len(states)),
        out_specs=[vmem_spec] * len(outs),
        scratch_shapes=[
            pltpu.VMEM((nq, *acc_shape), jnp.float32),
            pltpu.VMEM((nq, *m_shape), jnp.float32),
            pltpu.VMEM((nq, QB, HEADS_DEV * HD), jnp.bfloat16),
            pltpu.VMEM((nkv, 2 * KV_DEV, HD), jnp.bfloat16),
            pltpu.VMEM((KV_DEV, QB), jnp.float32),
            pltpu.VMEM((KV_DEV, QB), jnp.bfloat16),
            pltpu.SMEM(block_order.shape, jnp.int32),
            pltpu.SMEM((len(pairs) + 1,), jnp.int32),
            pltpu.SMEM((len(pairs) + 1,), jnp.int32),
            pltpu.SMEM((2 * len(pairs) + 1, 5), jnp.int32),
            pltpu.SMEM((nkv,), jnp.int32),
            pltpu.SemaphoreType.DMA,
            pltpu.SemaphoreType.DMA((nkv, 2)),
        ],
        compiler_params=pltpu.CompilerParams(vmem_limit_bytes=28 * 1024 * 1024),
        cost_estimate=pl.CostEstimate(
            flops=4 * len(pairs) * QROWS * KV_DEV * HD,
            bytes_accessed=nq * QROWS * HD * 4 + nkv * KV_DEV * HD * 4,
            transcendentals=len(pairs) * QROWS * KV_DEV,
        ),
        name="attend",
    )(
        block_order,
        *queries,
        *[blocks[step] for step in kv_steps],
        *[array for i in sorted(states) for array in states[i]],
    )
    return results if final else [tuple(results[2 * i : 2 * i + 2]) for i in range(nq)]


def pack(keys, values):
    pieces = values.reshape(KV_DEV // HD, HD, HD).swapaxes(1, 2).reshape(KV_DEV, HD)
    return jnp.concatenate([keys, pieces], axis=0)


def combine_kernel(*refs):
    parts, result = refs[:NZ], refs[NZ]
    stats = [part[QB:, :].astype(jnp.float32) for part in parts]
    for head in range(HEADS_DEV):
        logs = []
        for stat in stats:
            halves = []
            for half in range(2):
                rows = [stat_row(head, piece, half) for piece in range(3)]
                halves.append(sum(stat[r : r + 1, :] for r in rows))
            logs.append(jnp.concatenate(halves, axis=1))
        top = logs[0]
        for log in logs[1:]:
            top = jnp.maximum(top, log)
        weights = [jnp.exp2(log - top) for log in logs]
        share = 1.0 / sum(weights)
        columns = slice(head * HD, (head + 1) * HD)
        gathered = jnp.zeros((QB, HD), jnp.float32)
        for weight, part in zip(weights, parts):
            across = jnp.broadcast_to(weight * share, (HD, QB)).T
            gathered = gathered + across * part[:QB, columns].astype(jnp.float32)
        result[:, columns] = gathered.astype(jnp.bfloat16)


def combine(parts):
    vmem_spec = pl.BlockSpec(memory_space=pltpu.VMEM)
    return pl.pallas_call(
        combine_kernel,
        out_shape=jax.ShapeDtypeStruct((QB, HEADS_DEV * HD), jnp.bfloat16),
        in_specs=[vmem_spec] * NZ,
        out_specs=vmem_spec,
        compiler_params=pltpu.CompilerParams(vmem_limit_bytes=32 * 1024 * 1024),
        cost_estimate=pl.CostEstimate(
            flops=8 * NZ * QROWS * HD,
            bytes_accessed=(NZ + 1) * QROWS * HD * 2,
            transcendentals=NZ * QROWS,
        ),
        name="combine",
    )(*parts)


def every(queries, keys):
    return tuple((qi, kj) for qi in queries for kj in keys)


def body(queries, keys, values, block_order):
    def key_block(step):
        return lax.ppermute(own, "x", ring(4, -step))

    def query_block(value, step):
        return lax.ppermute(value, "z", ring(4, -step))

    def give_back(part, step):
        return lax.ppermute(part, "z", ring(4, step))

    own = pack(keys, values)
    blocks = {(0, 0): own, (1, 0): key_block(1), (3, 0): key_block(3), (0, 1): swap_core(own)}
    back, ahead = query_block(queries, 3), query_block(queries, 1)
    far, back, ahead = lax.optimization_barrier((queries, back, ahead))
    far = query_block(far, 2)
    near = blocks[1, 0], blocks[3, 0]
    own, back, ahead, near = lax.optimization_barrier((own, back, ahead, near))
    blocks[1, 0], blocks[3, 0] = near
    blocks[2, 0] = key_block(2)
    for step in (1, 3):
        blocks[step, 1] = swap_core(blocks[step, 0])
    *states, own_state = attend(
        block_order,
        [back, ahead, queries],
        FIRST + (0,),
        blocks,
        HERE,
        every((0, 1, 2), range(4)),
        final=False,
        own_early=True,
    )
    states, far, blocks[2, 0] = lax.optimization_barrier((states, far, blocks[2, 0]))
    blocks[2, 1] = swap_core(blocks[2, 0])
    to_back, to_ahead = attend(
        block_order,
        [back, ahead],
        FIRST,
        blocks,
        LATER + HERE,
        every((0, 1), range(4)),
        dict(enumerate(states)),
    )
    to_back, to_ahead, far = lax.optimization_barrier((to_back, to_ahead, far))
    here = [give_back(to_back, 3), give_back(to_ahead, 1)]
    (to_far,) = attend(block_order, [far], (2,), blocks, HERE + LATER, every((0,), range(8)))
    to_far, queries, here = lax.optimization_barrier((to_far, queries, here))
    here.append(give_back(to_far, 2))
    (own_part,) = attend(
        block_order,
        [queries],
        (0,),
        blocks,
        LATER + HERE,
        every((0,), range(8)),
        {0: own_state},
        own_early=False,
    )
    return combine([own_part, *here])


def solution(mesh):
    split = Mesh(mesh.devices.reshape(4, 4, 2, 4), ("x", "z", "core", "qh"))
    ctx = ("x", "z", "core")
    in_specs = (P(ctx, "qh"), P(ctx, None), P(ctx, None), P())
    out_specs = P(ctx, "qh")
    return jax.shard_map(body, mesh=split, in_specs=in_specs, out_specs=out_specs, check_vma=False)
```

```python
import math

import jax
import jax.numpy as jnp
from jax import lax
from jax.experimental import pallas as pl
from jax.experimental.pallas import tpu as pltpu
from jax.sharding import Mesh, PartitionSpec as P

HD = 128
KV_DEV = 1024
QB = 512
HEADS_DEV = 2
QROWS = QB * HEADS_DEV
SUMS = 16
SAMPLE = 128
PART = 512
FIRST_BLOCK = 16
SCALE = 1.4426950408889634 / math.sqrt(HD)
LOW = -1e30
SAFE = 2.0**100
NZ = 4
HERE = ((0, 0), (0, 1), (1, 0), (3, 0))
LATER = ((1, 1), (3, 1), (2, 0), (2, 1))
FIRST = (3, 1)
EARLY_PAIRS = 10
LATE_PAIRS = 5
STATS = 16
NT = (((1,), (1,)), ((), ()))


def ring(size, step):
    return [(i, (i + step) % size) for i in range(size)]


def swap_core(value):
    return lax.ppermute(value, "core", [(0, 1), (1, 0)])


def scores(keys, q):
    return lax.dot_general(keys, q, NT, preferred_element_type=jnp.float32)


def visible_keys(order, block, first, count):
    k_pos = block * KV_DEV + first + lax.broadcasted_iota(jnp.int32, (count, QB), 0)
    q_pos = FIRST_BLOCK * KV_DEV + order * QB + lax.broadcasted_iota(jnp.int32, (count, QB), 1)
    return k_pos <= q_pos


def q_head(q_s, qi, head):
    return q_s[qi, :, head * HD : (head + 1) * HD]


def keys_of(kv_s, kj):
    return kv_s[kj, :KV_DEV, :]


def values_product(kv_s, kj, p, first=0):
    count = p.shape[0]
    starts = [KV_DEV + first + i for i in range(0, count, HD)]
    across = jnp.concatenate([kv_s[kj, pl.ds(i, HD), :] for i in starts], axis=1)
    tall = jnp.concatenate([across, jnp.ones((SUMS, count), jnp.bfloat16)], axis=0)
    return jnp.dot(tall, p, preferred_element_type=jnp.float32)


def stat_row(head, piece, half):
    return (head * 3 + piece) * 2 + half


def probabilities(s, ref_point):
    return jnp.exp2(s * SCALE - ref_point)


def masked_step(q_s, kv_s, m_s, acc_s, qi, kj, order, block, first):
    visible = visible_keys(order, block, first, QB)
    for head in range(HEADS_DEV):
        s = scores(kv_s[kj, pl.ds(first, QB), :], q_head(q_s, qi, head))
        p = probabilities(s, m_s[qi, head, :1, :])
        p = jnp.where(visible, p, 0.0).astype(jnp.bfloat16)
        acc_s[qi, head] += values_product(kv_s, kj, p, first)


def running_step(q_s, kv_s, m_s, acc_s, qi, kj, order, block, first):
    visible = visible_keys(order, block, first, PART)
    for head in range(HEADS_DEV):
        s = scores(kv_s[kj, pl.ds(first, PART), :], q_head(q_s, qi, head))
        s = jnp.where(visible, s * SCALE, LOW)
        m_old = m_s[qi, head]
        m_new = jnp.maximum(m_old, jnp.max(s, axis=0, keepdims=True))
        p = jnp.where(visible, jnp.exp2(s - m_new[:1]), 0.0).astype(jnp.bfloat16)
        m_s[qi, head] = m_new
        acc_s[qi, head] = acc_s[qi, head] * jnp.exp2(m_old - m_new)[:1] + values_product(
            kv_s, kj, p, first
        )


def attend_kernel(z_steps, kv_steps, pairs, resumed, final, own_early, order_in, *refs):
    nq, nkv = len(z_steps), len(kv_steps)
    now = 1 + max(kj for _, kj in pairs)
    refs = list(refs)
    q_in = [refs.pop(0) for _ in range(nq)]
    kv_in = [refs.pop(0) for _ in range(nkv)]
    state_in = {i: (refs.pop(0), refs.pop(0)) for i in resumed}
    if final:
        outs = [refs.pop(0) for _ in range(nq)]
    else:
        state_out = [(refs.pop(0), refs.pop(0)) for _ in range(nq)]
    acc_s, m_s, q_s, kv_s, s_s, p_s, order_ref, list_q, list_k, edge_s, block_s = refs[:11]
    order_sem, kv_sem = refs[11:]
    x = lax.axis_index("x")
    z = lax.axis_index("z")
    core = lax.axis_index("core")

    def kv_copy(j, half, source=1):
        rows = pl.ds(half * KV_DEV, KV_DEV)
        return pltpu.make_async_copy(
            kv_in[source].at[rows, :], kv_s.at[j, rows, :], kv_sem.at[j, half]
        )

    order_copy = pltpu.make_async_copy(order_in, order_ref, order_sem)
    kv_copies = [kv_copy(j, half, j) for j in range(nkv) for half in range(2)]
    for copy in [order_copy, *kv_copies[2 : 2 * now]]:
        copy.start()
    for i in range(nq):
        q_s[i] = q_in[i][...]
    kv_s[0] = kv_in[0][...]
    acc_s[...] = jnp.zeros(acc_s.shape, jnp.float32)
    p_s[...] = jnp.zeros(p_s.shape, jnp.bfloat16)
    for i in range(nq):
        if i in resumed:
            m_s[i] = state_in[i][1][...]
            continue
        for head in range(HEADS_DEV):
            s = scores(kv_s[0, :SAMPLE, :], q_head(q_s, i, head))
            top = jnp.max(s, axis=0, keepdims=True) * SCALE
            m_s[i, head] = jnp.broadcast_to(top, (8, QB))
    order_copy.wait()

    def order_at(step):
        return order_ref[x * 8 + lax.rem(z + step, 4) * 2 + core]

    def block_at(step):
        return lax.rem(x + step[0], 4) * 8 + z * 2 + lax.rem(core + step[1], 2)

    def reaches(order, block):
        return block <= FIRST_BLOCK + order // 2

    orders = [order_at(step) for step in z_steps]
    blocks = [block_at(step) for step in kv_steps]
    taken = {}
    if own_early is not None:
        load = jnp.int32(0)
        for z_step in FIRST:
            for step in HERE:
                load += reaches(order_at(z_step), block_at(step)).astype(jnp.int32)
        left = jnp.int32(0)
        for step in HERE + LATER:
            left += reaches(order_at(0), block_at(step)).astype(jnp.int32)
        for step in HERE:
            early = reaches(order_at(0), block_at(step)) & (load < EARLY_PAIRS) & (left > LATE_PAIRS)
            load += early.astype(jnp.int32)
            left -= early.astype(jnp.int32)
            taken[step] = early if own_early else jnp.logical_not(early)
    for j, block in enumerate(blocks):
        block_s[j] = block
    count = edges = jnp.int32(0)
    for qi, kj in pairs:
        last = FIRST_BLOCK + orders[qi] // 2
        list_q[count] = qi
        list_k[count] = kj
        mine = taken.get(kv_steps[kj], True) if z_steps[qi] == 0 else True
        count += ((blocks[kj] < last) & mine).astype(jnp.int32)
        for first in (0, QB):
            for column, value in enumerate((qi, kj, orders[qi], blocks[kj], first)):
                edge_s[edges, column] = value
            seen = (blocks[kj] == last) & mine
            if first > 0:
                seen = seen & (lax.rem(orders[qi], 2) == 1)
            edges += seen.astype(jnp.int32)

    def wait_upto(done, needed):
        def wait_one(j, carry):
            for half in range(2):
                kv_copy(j, half).wait()
            return carry

        lax.fori_loop(done, needed + 1, wait_one, 0)
        return jnp.maximum(done, needed + 1)

    parts = range(0, KV_DEV, PART)

    def pair(t, carry):
        q_old, k_old, here = carry
        qi, kj = list_q[t], list_k[t]
        after = jnp.minimum(t + 1, count - 1)
        q_next, k_next = list_q[after], list_k[after]
        here = wait_upto(here, k_next)
        s = [s_s[i : i + PART, :] for i in parts]
        p_old = [p_s[i : i + PART, :] for i in parts]
        for head in range(HEADS_DEV):
            if head + 1 < HEADS_DEV:
                q_then, k_then, head_then = qi, kj, head + 1
            else:
                q_then, k_then, head_then = q_next, k_next, 0
            if head > 0:
                q_old, k_old = qi, kj
            head_old = (head - 1) % HEADS_DEV
            ref_point = m_s[qi, head, :1, :]
            s_next, p_new, total = [], [], acc_s[q_old, head_old]
            for n, i in enumerate(parts):
                s_next.append(
                    scores(kv_s[k_then, i : i + PART, :], q_head(q_s, q_then, head_then))
                )
                p_new.append(probabilities(s[n], ref_point).astype(jnp.bfloat16))
                total = total + values_product(kv_s, k_old, p_old[n], i)
            acc_s[q_old, head_old] = total
            s, p_old = s_next, p_new
        for n, i in enumerate(parts):
            s_s[i : i + PART, :] = s[n]
            p_s[i : i + PART, :] = p_old[n]
        return qi, kj, here

    here = wait_upto(jnp.int32(1), list_k[0])
    s_s[...] = scores(keys_of(kv_s, list_k[0]), q_head(q_s, list_q[0], 0))
    q_last, k_last, here = lax.fori_loop(0, count, pair, (list_q[0], list_k[0], here))
    wait_upto(here, jnp.int32(now - 1))

    def edge(t, carry):
        qi, kj, order, block = [edge_s[t, column] for column in range(4)]
        first = pl.multiple_of(edge_s[t, 4], QB)
        masked_step(q_s, kv_s, m_s, acc_s, qi, kj, order, block, first)
        return carry

    lax.fori_loop(0, edges, edge, 0)
    q_last = 0 if nq == 1 else q_last
    acc_s[q_last, HEADS_DEV - 1] += values_product(kv_s, k_last, p_s[...])
    if not final:
        for i in range(nq):
            state_out[i][0][...] = acc_s[i]
            state_out[i][1][...] = m_s[i]
        return
    for i in resumed:
        acc_s[i] += state_in[i][0][...]

    row = lax.broadcasted_iota(jnp.int32, (STATS, HEADS_DEV * HD), 0)

    def finish(i):
        logs = jnp.zeros((STATS, HEADS_DEV * HD), jnp.float32)
        for head in range(HEADS_DEV):
            total = acc_s[i, head, HD : HD + 1, :]
            outs[i][:QB, head * HD : (head + 1) * HD] = (
                (acc_s[i, head, :HD, :] * (1.0 / total)).T.astype(jnp.bfloat16)
            )
            rest = m_s[i, head, :1, :] + jnp.log2(total)
            for piece in range(3):
                part = rest.astype(jnp.bfloat16).astype(jnp.float32)
                for half in range(2):
                    columns = part[:, half * HEADS_DEV * HD : (half + 1) * HEADS_DEV * HD]
                    logs = jnp.where(row == stat_row(head, piece, half), columns, logs)
                rest = rest - part
        outs[i][QB:, :] = logs.astype(jnp.bfloat16)

    def redo(qi, order):
        m_s[qi] = jnp.full(m_s.shape[1:], LOW, jnp.float32)
        acc_s[qi] = jnp.zeros(acc_s.shape[1:], jnp.float32)

        def step(t, carry):
            kj = t // (KV_DEV // PART)
            first = pl.multiple_of(lax.rem(t, KV_DEV // PART) * PART, PART)
            block = block_s[kj]

            @pl.when(block <= FIRST_BLOCK + order // 2)
            def _():
                running_step(q_s, kv_s, m_s, acc_s, qi, kj, order, block, first)

            return carry

        lax.fori_loop(0, nkv * (KV_DEV // PART), step, 0)

    for i in range(nq):
        finish(i)
    totals = acc_s[:, :, HD : HD + 8, :]
    bad = jnp.max(jnp.where((totals > 1.0 / SAFE) & (totals < SAFE), 0.0, 1.0))

    @pl.when(bad > 0.0)
    def _():
        for copy in kv_copies[2 * now :]:
            copy.start()
        for copy in kv_copies[2 * now :]:
            copy.wait()
        for i in range(nq):
            redo(i, orders[i])
            finish(i)


def attend(
    block_order,
    queries,
    z_steps,
    blocks,
    kv_steps,
    pairs,
    states=None,
    final=True,
    own_early=None,
):
    states = states or {}
    nq, nkv = len(queries), len(kv_steps)
    any_spec = pl.BlockSpec(memory_space=pl.ANY)
    vmem_spec = pl.BlockSpec(memory_space=pltpu.VMEM)
    acc_shape, m_shape = (HEADS_DEV, HD + SUMS, QB), (HEADS_DEV, 8, QB)
    if final:
        outs = [jax.ShapeDtypeStruct((QB + STATS, HEADS_DEV * HD), jnp.bfloat16)] * nq
    else:
        outs = [jax.ShapeDtypeStruct(shape, jnp.float32) for shape in (acc_shape, m_shape)] * nq
    results = pl.pallas_call(
        lambda *refs: attend_kernel(
            z_steps, kv_steps, pairs, sorted(states), final, own_early, *refs
        ),
        out_shape=outs,
        in_specs=[any_spec]
        + [vmem_spec] * (nq + 1)
        + [any_spec] * (nkv - 1)
        + [vmem_spec] * (2 * len(states)),
        out_specs=[vmem_spec] * len(outs),
        scratch_shapes=[
            pltpu.VMEM((nq, *acc_shape), jnp.float32),
            pltpu.VMEM((nq, *m_shape), jnp.float32),
            pltpu.VMEM((nq, QB, HEADS_DEV * HD), jnp.bfloat16),
            pltpu.VMEM((nkv, 2 * KV_DEV, HD), jnp.bfloat16),
            pltpu.VMEM((KV_DEV, QB), jnp.float32),
            pltpu.VMEM((KV_DEV, QB), jnp.bfloat16),
            pltpu.SMEM(block_order.shape, jnp.int32),
            pltpu.SMEM((len(pairs) + 1,), jnp.int32),
            pltpu.SMEM((len(pairs) + 1,), jnp.int32),
            pltpu.SMEM((2 * len(pairs) + 1, 5), jnp.int32),
            pltpu.SMEM((nkv,), jnp.int32),
            pltpu.SemaphoreType.DMA,
            pltpu.SemaphoreType.DMA((nkv, 2)),
        ],
        compiler_params=pltpu.CompilerParams(vmem_limit_bytes=28 * 1024 * 1024),
        cost_estimate=pl.CostEstimate(
            flops=4 * len(pairs) * QROWS * KV_DEV * HD,
            bytes_accessed=nq * QROWS * HD * 4 + nkv * KV_DEV * HD * 4,
            transcendentals=len(pairs) * QROWS * KV_DEV,
        ),
        name="attend",
    )(
        block_order,
        *queries,
        *[blocks[step] for step in kv_steps],
        *[array for i in sorted(states) for array in states[i]],
    )
    return results if final else [tuple(results[2 * i : 2 * i + 2]) for i in range(nq)]


def pack(keys, values):
    pieces = values.reshape(KV_DEV // HD, HD, HD).swapaxes(1, 2).reshape(KV_DEV, HD)
    return jnp.concatenate([keys, pieces], axis=0)


def combine_kernel(*refs):
    parts, result = refs[:NZ], refs[NZ]
    stats = [part[QB:, :].astype(jnp.float32) for part in parts]
    for head in range(HEADS_DEV):
        logs = []
        for stat in stats:
            halves = []
            for half in range(2):
                rows = [stat_row(head, piece, half) for piece in range(3)]
                halves.append(sum(stat[r : r + 1, :] for r in rows))
            logs.append(jnp.concatenate(halves, axis=1))
        top = logs[0]
        for log in logs[1:]:
            top = jnp.maximum(top, log)
        weights = [jnp.exp2(log - top) for log in logs]
        share = 1.0 / sum(weights)
        columns = slice(head * HD, (head + 1) * HD)
        gathered = jnp.zeros((QB, HD), jnp.float32)
        for weight, part in zip(weights, parts):
            across = jnp.broadcast_to(weight * share, (HD, QB)).T
            gathered = gathered + across * part[:QB, columns].astype(jnp.float32)
        result[:, columns] = gathered.astype(jnp.bfloat16)


def combine(parts):
    vmem_spec = pl.BlockSpec(memory_space=pltpu.VMEM)
    return pl.pallas_call(
        combine_kernel,
        out_shape=jax.ShapeDtypeStruct((QB, HEADS_DEV * HD), jnp.bfloat16),
        in_specs=[vmem_spec] * NZ,
        out_specs=vmem_spec,
        compiler_params=pltpu.CompilerParams(vmem_limit_bytes=32 * 1024 * 1024),
        cost_estimate=pl.CostEstimate(
            flops=8 * NZ * QROWS * HD,
            bytes_accessed=(NZ + 1) * QROWS * HD * 2,
            transcendentals=NZ * QROWS,
        ),
        name="combine",
    )(*parts)


def every(queries, keys):
    return tuple((qi, kj) for qi in queries for kj in keys)


def body(queries, keys, values, block_order):
    def key_block(step):
        return lax.ppermute(own, "x", ring(4, -step))

    def query_block(value, step):
        return lax.ppermute(value, "z", ring(4, -step))

    def give_back(part, step):
        return lax.ppermute(part, "z", ring(4, step))

    own = pack(keys, values)
    blocks = {(0, 0): own, (1, 0): key_block(1), (3, 0): key_block(3), (0, 1): swap_core(own)}
    back, ahead = query_block(queries, 3), query_block(queries, 1)
    far, back, ahead = lax.optimization_barrier((queries, back, ahead))
    far = query_block(far, 2)
    near = blocks[1, 0], blocks[3, 0]
    own, back, ahead, near = lax.optimization_barrier((own, back, ahead, near))
    blocks[1, 0], blocks[3, 0] = near
    blocks[2, 0] = key_block(2)
    for step in (1, 3):
        blocks[step, 1] = swap_core(blocks[step, 0])
    *states, own_state = attend(
        block_order,
        [back, ahead, queries],
        FIRST + (0,),
        blocks,
        HERE,
        every((0, 1, 2), range(4)),
        final=False,
        own_early=True,
    )
    states, far, blocks[2, 0] = lax.optimization_barrier((states, far, blocks[2, 0]))
    blocks[2, 1] = swap_core(blocks[2, 0])
    to_back, to_ahead = attend(
        block_order,
        [back, ahead],
        FIRST,
        blocks,
        LATER + HERE,
        every((0, 1), range(4)),
        dict(enumerate(states)),
    )
    to_back, to_ahead, far = lax.optimization_barrier((to_back, to_ahead, far))
    here = [give_back(to_back, 3), give_back(to_ahead, 1)]
    (to_far,) = attend(block_order, [far], (2,), blocks, HERE + LATER, every((0,), range(8)))
    to_far, queries, here = lax.optimization_barrier((to_far, queries, here))
    here.append(give_back(to_far, 2))
    (own_part,) = attend(
        block_order,
        [queries],
        (0,),
        blocks,
        LATER + HERE,
        every((0,), range(8)),
        {0: own_state},
        own_early=False,
    )
    return combine([own_part, *here])


def solution(mesh):
    split = Mesh(mesh.devices.reshape(4, 4, 2, 4), ("x", "z", "core", "qh"))
    ctx = ("x", "z", "core")
    in_specs = (P(ctx, "qh"), P(ctx, None), P(ctx, None), P())
    out_specs = P(ctx, "qh")
    return jax.shard_map(body, mesh=split, in_specs=in_specs, out_specs=out_specs, check_vma=False)
```

```python
import math

import jax
import jax.numpy as jnp
from jax import lax
from jax.experimental import pallas as pl
from jax.experimental.pallas import tpu as pltpu
from jax.sharding import Mesh, PartitionSpec as P

HD = 128
KV_DEV = 1024
QB = 512
HEADS_DEV = 2
QROWS = QB * HEADS_DEV
SUMS = 16
SAMPLE = 128
PART = 512
FIRST_BLOCK = 16
SCALE = 1.4426950408889634 / math.sqrt(HD)
LOW = -1e30
SAFE = 2.0**100
NZ = 4
HERE = ((0, 0), (0, 1), (1, 0), (3, 0))
LATER = ((1, 1), (3, 1), (2, 0), (2, 1))
FIRST = (3, 1)
EARLY_PAIRS = 10
STATS = 16
NT = (((1,), (1,)), ((), ()))


def ring(size, step):
    return [(i, (i + step) % size) for i in range(size)]


def swap_core(value):
    return lax.ppermute(value, "core", [(0, 1), (1, 0)])


def scores(keys, q):
    return lax.dot_general(keys, q, NT, preferred_element_type=jnp.float32)


def visible_keys(order, block, first, count):
    k_pos = block * KV_DEV + first + lax.broadcasted_iota(jnp.int32, (count, QB), 0)
    q_pos = FIRST_BLOCK * KV_DEV + order * QB + lax.broadcasted_iota(jnp.int32, (count, QB), 1)
    return k_pos <= q_pos


def q_head(q_s, qi, head):
    return q_s[qi, :, head * HD : (head + 1) * HD]


def keys_of(kv_s, kj):
    return kv_s[kj, :KV_DEV, :]


def values_product(kv_s, kj, p, first=0):
    count = p.shape[0]
    starts = [KV_DEV + first + i for i in range(0, count, HD)]
    across = jnp.concatenate([kv_s[kj, pl.ds(i, HD), :] for i in starts], axis=1)
    tall = jnp.concatenate([across, jnp.ones((SUMS, count), jnp.bfloat16)], axis=0)
    return jnp.dot(tall, p, preferred_element_type=jnp.float32)


def stat_row(head, piece):
    return head * 3 + piece


def probabilities(s, ref_point):
    return jnp.exp2(s * SCALE - ref_point)


def masked_step(q_s, kv_s, m_s, acc_s, qi, kj, order, block, first):
    visible = visible_keys(order, block, first, QB)
    for head in range(HEADS_DEV):
        s = scores(kv_s[kj, pl.ds(first, QB), :], q_head(q_s, qi, head))
        p = probabilities(s, m_s[qi, head, :1, :])
        p = jnp.where(visible, p, 0.0).astype(jnp.bfloat16)
        acc_s[qi, head] += values_product(kv_s, kj, p, first)


def running_step(q_s, kv_s, m_s, acc_s, qi, kj, order, block, first):
    visible = visible_keys(order, block, first, PART)
    for head in range(HEADS_DEV):
        s = scores(kv_s[kj, pl.ds(first, PART), :], q_head(q_s, qi, head))
        s = jnp.where(visible, s * SCALE, LOW)
        m_old = m_s[qi, head]
        m_new = jnp.maximum(m_old, jnp.max(s, axis=0, keepdims=True))
        p = jnp.where(visible, jnp.exp2(s - m_new[:1]), 0.0).astype(jnp.bfloat16)
        m_s[qi, head] = m_new
        acc_s[qi, head] = acc_s[qi, head] * jnp.exp2(m_old - m_new)[:1] + values_product(
            kv_s, kj, p, first
        )


def attend_kernel(z_steps, kv_steps, pairs, resumed, final, own_early, order_in, *refs):
    nq, nkv = len(z_steps), len(kv_steps)
    now = 1 + max(kj for _, kj in pairs)
    refs = list(refs)
    q_in = [refs.pop(0) for _ in range(nq)]
    kv_in = [refs.pop(0) for _ in range(nkv)]
    state_in = {i: (refs.pop(0), refs.pop(0)) for i in resumed}
    if final:
        outs = [refs.pop(0) for _ in range(nq)]
    else:
        state_out = [(refs.pop(0), refs.pop(0)) for _ in range(nq)]
    acc_s, m_s, q_s, kv_s, s_s, p_s, order_ref, list_q, list_k, edge_s, block_s = refs[:11]
    order_sem, kv_sem = refs[11:]
    x = lax.axis_index("x")
    z = lax.axis_index("z")
    core = lax.axis_index("core")

    def kv_copy(j, half, source=1):
        rows = pl.ds(half * KV_DEV, KV_DEV)
        return pltpu.make_async_copy(
            kv_in[source].at[rows, :], kv_s.at[j, rows, :], kv_sem.at[j, half]
        )

    order_copy = pltpu.make_async_copy(order_in, order_ref, order_sem)
    kv_copies = [kv_copy(j, half, j) for j in range(nkv) for half in range(2)]
    for copy in [order_copy, *kv_copies[2 : 2 * now]]:
        copy.start()
    for i in range(nq):
        q_s[i] = q_in[i][...]
    kv_s[0] = kv_in[0][...]
    acc_s[...] = jnp.zeros(acc_s.shape, jnp.float32)
    p_s[...] = jnp.zeros(p_s.shape, jnp.bfloat16)
    for i in range(nq):
        if i in resumed:
            m_s[i] = state_in[i][1][...]
            continue
        for head in range(HEADS_DEV):
            s = scores(kv_s[0, :SAMPLE, :], q_head(q_s, i, head))
            top = jnp.max(s, axis=0, keepdims=True) * SCALE
            m_s[i, head] = jnp.broadcast_to(top, (8, QB))
    order_copy.wait()

    def order_at(step):
        return order_ref[x * 8 + lax.rem(z + step, 4) * 2 + core]

    def block_at(step):
        return lax.rem(x + step[0], 4) * 8 + z * 2 + lax.rem(core + step[1], 2)

    def reaches(order, block):
        return block <= FIRST_BLOCK + order // 2

    orders = [order_at(step) for step in z_steps]
    blocks = [block_at(step) for step in kv_steps]
    taken = {}
    if own_early is not None:
        load = jnp.int32(0)
        for z_step in FIRST:
            for step in HERE:
                load += reaches(order_at(z_step), block_at(step)).astype(jnp.int32)
        for step in HERE:
            early = reaches(order_at(0), block_at(step)) & (load < EARLY_PAIRS)
            load += early.astype(jnp.int32)
            taken[step] = early if own_early else jnp.logical_not(early)
    for j, block in enumerate(blocks):
        block_s[j] = block
    count = edges = jnp.int32(0)
    for qi, kj in pairs:
        last = FIRST_BLOCK + orders[qi] // 2
        list_q[count] = qi
        list_k[count] = kj
        mine = taken.get(kv_steps[kj], True) if z_steps[qi] == 0 else True
        count += ((blocks[kj] < last) & mine).astype(jnp.int32)
        for first in (0, QB):
            for column, value in enumerate((qi, kj, orders[qi], blocks[kj], first)):
                edge_s[edges, column] = value
            seen = (blocks[kj] == last) & mine
            if first > 0:
                seen = seen & (lax.rem(orders[qi], 2) == 1)
            edges += seen.astype(jnp.int32)

    def wait_upto(done, needed):
        def wait_one(j, carry):
            for half in range(2):
                kv_copy(j, half).wait()
            return carry

        lax.fori_loop(done, needed + 1, wait_one, 0)
        return jnp.maximum(done, needed + 1)

    parts = range(0, KV_DEV, PART)

    def pair(t, carry):
        q_old, k_old, here = carry
        qi, kj = list_q[t], list_k[t]
        after = jnp.minimum(t + 1, count - 1)
        q_next, k_next = list_q[after], list_k[after]
        here = wait_upto(here, k_next)
        s = [s_s[i : i + PART, :] for i in parts]
        p_old = [p_s[i : i + PART, :] for i in parts]
        for head in range(HEADS_DEV):
            if head + 1 < HEADS_DEV:
                q_then, k_then, head_then = qi, kj, head + 1
            else:
                q_then, k_then, head_then = q_next, k_next, 0
            if head > 0:
                q_old, k_old = qi, kj
            head_old = (head - 1) % HEADS_DEV
            ref_point = m_s[qi, head, :1, :]
            s_next, p_new, total = [], [], acc_s[q_old, head_old]
            for n, i in enumerate(parts):
                s_next.append(
                    scores(kv_s[k_then, i : i + PART, :], q_head(q_s, q_then, head_then))
                )
                p_new.append(probabilities(s[n], ref_point).astype(jnp.bfloat16))
                total = total + values_product(kv_s, k_old, p_old[n], i)
            acc_s[q_old, head_old] = total
            s, p_old = s_next, p_new
        for n, i in enumerate(parts):
            s_s[i : i + PART, :] = s[n]
            p_s[i : i + PART, :] = p_old[n]
        return qi, kj, here

    here = wait_upto(jnp.int32(1), list_k[0])
    s_s[...] = scores(keys_of(kv_s, list_k[0]), q_head(q_s, list_q[0], 0))
    q_last, k_last, here = lax.fori_loop(0, count, pair, (list_q[0], list_k[0], here))
    wait_upto(here, jnp.int32(now - 1))

    def edge(t, carry):
        qi, kj, order, block = [edge_s[t, column] for column in range(4)]
        first = pl.multiple_of(edge_s[t, 4], QB)
        masked_step(q_s, kv_s, m_s, acc_s, qi, kj, order, block, first)
        return carry

    lax.fori_loop(0, edges, edge, 0)
    q_last = 0 if nq == 1 else q_last
    acc_s[q_last, HEADS_DEV - 1] += values_product(kv_s, k_last, p_s[...])
    if not final:
        for i in range(nq):
            state_out[i][0][...] = acc_s[i]
            state_out[i][1][...] = m_s[i]
        return
    for i in resumed:
        acc_s[i] += state_in[i][0][...]

    row = lax.broadcasted_iota(jnp.int32, (STATS, QB), 0)

    def finish(i):
        logs = jnp.zeros((STATS, QB), jnp.float32)
        for head in range(HEADS_DEV):
            total = acc_s[i, head, HD : HD + 1, :]
            outs[i][head * HD : (head + 1) * HD, :] = (
                acc_s[i, head, :HD, :] * (1.0 / total)
            ).astype(jnp.bfloat16)
            rest = m_s[i, head, :1, :] + jnp.log2(total)
            for piece in range(3):
                part = rest.astype(jnp.bfloat16).astype(jnp.float32)
                logs = jnp.where(row == stat_row(head, piece), part, logs)
                rest = rest - part
        outs[i][HEADS_DEV * HD :, :] = logs.astype(jnp.bfloat16)

    def redo(qi, order):
        m_s[qi] = jnp.full(m_s.shape[1:], LOW, jnp.float32)
        acc_s[qi] = jnp.zeros(acc_s.shape[1:], jnp.float32)

        def step(t, carry):
            kj = t // (KV_DEV // PART)
            first = pl.multiple_of(lax.rem(t, KV_DEV // PART) * PART, PART)
            block = block_s[kj]

            @pl.when(block <= FIRST_BLOCK + order // 2)
            def _():
                running_step(q_s, kv_s, m_s, acc_s, qi, kj, order, block, first)

            return carry

        lax.fori_loop(0, nkv * (KV_DEV // PART), step, 0)

    for i in range(nq):
        finish(i)
    totals = acc_s[:, :, HD : HD + 8, :]
    bad = jnp.max(jnp.where((totals > 1.0 / SAFE) & (totals < SAFE), 0.0, 1.0))

    @pl.when(bad > 0.0)
    def _():
        for copy in kv_copies[2 * now :]:
            copy.start()
        for copy in kv_copies[2 * now :]:
            copy.wait()
        for i in range(nq):
            redo(i, orders[i])
            finish(i)


def attend(
    block_order,
    queries,
    z_steps,
    blocks,
    kv_steps,
    pairs,
    states=None,
    final=True,
    own_early=None,
):
    states = states or {}
    nq, nkv = len(queries), len(kv_steps)
    any_spec = pl.BlockSpec(memory_space=pl.ANY)
    vmem_spec = pl.BlockSpec(memory_space=pltpu.VMEM)
    acc_shape, m_shape = (HEADS_DEV, HD + SUMS, QB), (HEADS_DEV, 8, QB)
    if final:
        outs = [jax.ShapeDtypeStruct((HEADS_DEV * HD + STATS, QB), jnp.bfloat16)] * nq
    else:
        outs = [jax.ShapeDtypeStruct(shape, jnp.float32) for shape in (acc_shape, m_shape)] * nq
    results = pl.pallas_call(
        lambda *refs: attend_kernel(
            z_steps, kv_steps, pairs, sorted(states), final, own_early, *refs
        ),
        out_shape=outs,
        in_specs=[any_spec]
        + [vmem_spec] * (nq + 1)
        + [any_spec] * (nkv - 1)
        + [vmem_spec] * (2 * len(states)),
        out_specs=[vmem_spec] * len(outs),
        scratch_shapes=[
            pltpu.VMEM((nq, *acc_shape), jnp.float32),
            pltpu.VMEM((nq, *m_shape), jnp.float32),
            pltpu.VMEM((nq, QB, HEADS_DEV * HD), jnp.bfloat16),
            pltpu.VMEM((nkv, 2 * KV_DEV, HD), jnp.bfloat16),
            pltpu.VMEM((KV_DEV, QB), jnp.float32),
            pltpu.VMEM((KV_DEV, QB), jnp.bfloat16),
            pltpu.SMEM(block_order.shape, jnp.int32),
            pltpu.SMEM((len(pairs) + 1,), jnp.int32),
            pltpu.SMEM((len(pairs) + 1,), jnp.int32),
            pltpu.SMEM((2 * len(pairs) + 1, 5), jnp.int32),
            pltpu.SMEM((nkv,), jnp.int32),
            pltpu.SemaphoreType.DMA,
            pltpu.SemaphoreType.DMA((nkv, 2)),
        ],
        compiler_params=pltpu.CompilerParams(vmem_limit_bytes=28 * 1024 * 1024),
        cost_estimate=pl.CostEstimate(
            flops=4 * len(pairs) * QROWS * KV_DEV * HD,
            bytes_accessed=nq * QROWS * HD * 4 + nkv * KV_DEV * HD * 4,
            transcendentals=len(pairs) * QROWS * KV_DEV,
        ),
        name="attend",
    )(
        block_order,
        *queries,
        *[blocks[step] for step in kv_steps],
        *[array for i in sorted(states) for array in states[i]],
    )
    return results if final else [tuple(results[2 * i : 2 * i + 2]) for i in range(nq)]


def pack(keys, values):
    pieces = values.reshape(KV_DEV // HD, HD, HD).swapaxes(1, 2).reshape(KV_DEV, HD)
    return jnp.concatenate([keys, pieces], axis=0)


def combine_kernel(*refs):
    parts, result = refs[:NZ], refs[NZ]
    stats = [part[HEADS_DEV * HD :, :].astype(jnp.float32) for part in parts]
    for head in range(HEADS_DEV):
        rows = [stat_row(head, piece) for piece in range(3)]
        logs = [sum(stat[r : r + 1, :] for r in rows) for stat in stats]
        top = logs[0]
        for log in logs[1:]:
            top = jnp.maximum(top, log)
        weights = [jnp.exp2(log - top) for log in logs]
        share = 1.0 / sum(weights)
        columns = slice(head * HD, (head + 1) * HD)
        gathered = jnp.zeros((HD, QB), jnp.float32)
        for weight, part in zip(weights, parts):
            gathered = gathered + weight * share * part[columns, :].astype(jnp.float32)
        result[:, columns] = gathered.T.astype(jnp.bfloat16)


def combine(parts):
    vmem_spec = pl.BlockSpec(memory_space=pltpu.VMEM)
    return pl.pallas_call(
        combine_kernel,
        out_shape=jax.ShapeDtypeStruct((QB, HEADS_DEV * HD), jnp.bfloat16),
        in_specs=[vmem_spec] * NZ,
        out_specs=vmem_spec,
        compiler_params=pltpu.CompilerParams(vmem_limit_bytes=32 * 1024 * 1024),
        cost_estimate=pl.CostEstimate(
            flops=8 * NZ * QROWS * HD,
            bytes_accessed=(NZ + 1) * QROWS * HD * 2,
            transcendentals=NZ * QROWS,
        ),
        name="combine",
    )(*parts)


def every(queries, keys):
    return tuple((qi, kj) for qi in queries for kj in keys)


def body(queries, keys, values, block_order):
    def key_block(step):
        return lax.ppermute(own, "x", ring(4, -step))

    def query_block(value, step):
        return lax.ppermute(value, "z", ring(4, -step))

    def give_back(part, step):
        return lax.ppermute(part, "z", ring(4, step))

    own = pack(keys, values)
    blocks = {(0, 0): own, (1, 0): key_block(1), (3, 0): key_block(3), (0, 1): swap_core(own)}
    back, ahead = query_block(queries, 3), query_block(queries, 1)
    far, back, ahead = lax.optimization_barrier((queries, back, ahead))
    far = query_block(far, 2)
    near = blocks[1, 0], blocks[3, 0]
    own, back, ahead, near = lax.optimization_barrier((own, back, ahead, near))
    blocks[1, 0], blocks[3, 0] = near
    blocks[2, 0] = key_block(2)
    for step in (1, 3):
        blocks[step, 1] = swap_core(blocks[step, 0])
    *states, own_state = attend(
        block_order,
        [back, ahead, queries],
        FIRST + (0,),
        blocks,
        HERE,
        every((0, 1, 2), range(4)),
        final=False,
        own_early=True,
    )
    states, far, blocks[2, 0] = lax.optimization_barrier((states, far, blocks[2, 0]))
    blocks[2, 1] = swap_core(blocks[2, 0])
    to_back, to_ahead = attend(
        block_order,
        [back, ahead],
        FIRST,
        blocks,
        LATER + HERE,
        every((0, 1), range(4)),
        dict(enumerate(states)),
    )
    to_back, to_ahead, far = lax.optimization_barrier((to_back, to_ahead, far))
    here = [give_back(to_back, 3), give_back(to_ahead, 1)]
    (to_far,) = attend(block_order, [far], (2,), blocks, HERE + LATER, every((0,), range(8)))
    to_far, queries, here = lax.optimization_barrier((to_far, queries, here))
    here.append(give_back(to_far, 2))
    (own_part,) = attend(
        block_order,
        [queries],
        (0,),
        blocks,
        LATER + HERE,
        every((0,), range(8)),
        {0: own_state},
        own_early=False,
    )
    return combine([own_part, *here])


def solution(mesh):
    split = Mesh(mesh.devices.reshape(4, 4, 2, 4), ("x", "z", "core", "qh"))
    ctx = ("x", "z", "core")
    in_specs = (P(ctx, "qh"), P(ctx, None), P(ctx, None), P())
    out_specs = P(ctx, "qh")
    return jax.shard_map(body, mesh=split, in_specs=in_specs, out_specs=out_specs, check_vma=False)
```

```python
import math

import jax
import jax.numpy as jnp
from jax import lax
from jax.experimental import pallas as pl
from jax.experimental.pallas import tpu as pltpu
from jax.sharding import Mesh, PartitionSpec as P

HD = 128
KV_DEV = 1024
QB = 512
HEADS_DEV = 2
QROWS = QB * HEADS_DEV
SUMS = 16
SAMPLE = 128
PART = 512
FIRST_BLOCK = 16
SCALE = 1.4426950408889634 / math.sqrt(HD)
LOW = -1e30
SAFE = 2.0**100
NZ = 4
HERE = ((0, 0), (0, 1), (1, 0), (3, 0))
LATER = ((1, 1), (3, 1), (2, 0), (2, 1))
FIRST = (3, 1)
EARLY_PAIRS = 9
STATS = 16
NT = (((1,), (1,)), ((), ()))


def ring(size, step):
    return [(i, (i + step) % size) for i in range(size)]


def swap_core(value):
    return lax.ppermute(value, "core", [(0, 1), (1, 0)])


def scores(keys, q):
    return lax.dot_general(keys, q, NT, preferred_element_type=jnp.float32)


def visible_keys(order, block, first, count):
    k_pos = block * KV_DEV + first + lax.broadcasted_iota(jnp.int32, (count, QB), 0)
    q_pos = FIRST_BLOCK * KV_DEV + order * QB + lax.broadcasted_iota(jnp.int32, (count, QB), 1)
    return k_pos <= q_pos


def q_head(q_s, qi, head):
    return q_s[qi, :, head * HD : (head + 1) * HD]


def keys_of(kv_s, kj):
    return kv_s[kj, :KV_DEV, :]


def values_product(kv_s, kj, p, first=0):
    count = p.shape[0]
    starts = [KV_DEV + first + i for i in range(0, count, HD)]
    across = jnp.concatenate([kv_s[kj, pl.ds(i, HD), :] for i in starts], axis=1)
    tall = jnp.concatenate([across, jnp.ones((SUMS, count), jnp.bfloat16)], axis=0)
    return jnp.dot(tall, p, preferred_element_type=jnp.float32)


def stat_row(head, piece):
    return head * 3 + piece


def probabilities(s, ref_point):
    return jnp.exp2(s * SCALE - ref_point)


def masked_step(q_s, kv_s, m_s, acc_s, qi, kj, order, block, first):
    visible = visible_keys(order, block, first, QB)
    for head in range(HEADS_DEV):
        s = scores(kv_s[kj, pl.ds(first, QB), :], q_head(q_s, qi, head))
        p = probabilities(s, m_s[qi, head, :1, :])
        p = jnp.where(visible, p, 0.0).astype(jnp.bfloat16)
        acc_s[qi, head] += values_product(kv_s, kj, p, first)


def running_step(q_s, kv_s, m_s, acc_s, qi, kj, order, block, first):
    visible = visible_keys(order, block, first, PART)
    for head in range(HEADS_DEV):
        s = scores(kv_s[kj, pl.ds(first, PART), :], q_head(q_s, qi, head))
        s = jnp.where(visible, s * SCALE, LOW)
        m_old = m_s[qi, head]
        m_new = jnp.maximum(m_old, jnp.max(s, axis=0, keepdims=True))
        p = jnp.where(visible, jnp.exp2(s - m_new[:1]), 0.0).astype(jnp.bfloat16)
        m_s[qi, head] = m_new
        acc_s[qi, head] = acc_s[qi, head] * jnp.exp2(m_old - m_new)[:1] + values_product(
            kv_s, kj, p, first
        )


def attend_kernel(z_steps, kv_steps, pairs, resumed, final, own_early, order_in, *refs):
    nq, nkv = len(z_steps), len(kv_steps)
    now = 1 + max(kj for _, kj in pairs)
    refs = list(refs)
    q_in = [refs.pop(0) for _ in range(nq)]
    kv_in = [refs.pop(0) for _ in range(nkv)]
    state_in = {i: (refs.pop(0), refs.pop(0)) for i in resumed}
    if final:
        outs = [refs.pop(0) for _ in range(nq)]
    else:
        state_out = [(refs.pop(0), refs.pop(0)) for _ in range(nq)]
    acc_s, m_s, q_s, kv_s, s_s, p_s, order_ref, list_q, list_k, edge_s, block_s = refs[:11]
    order_sem, kv_sem = refs[11:]
    x = lax.axis_index("x")
    z = lax.axis_index("z")
    core = lax.axis_index("core")

    def kv_copy(j, half, source=1):
        rows = pl.ds(half * KV_DEV, KV_DEV)
        return pltpu.make_async_copy(
            kv_in[source].at[rows, :], kv_s.at[j, rows, :], kv_sem.at[j, half]
        )

    order_copy = pltpu.make_async_copy(order_in, order_ref, order_sem)
    kv_copies = [kv_copy(j, half, j) for j in range(nkv) for half in range(2)]
    for copy in [order_copy, *kv_copies[2 : 2 * now]]:
        copy.start()
    for i in range(nq):
        q_s[i] = q_in[i][...]
    kv_s[0] = kv_in[0][...]
    acc_s[...] = jnp.zeros(acc_s.shape, jnp.float32)
    p_s[...] = jnp.zeros(p_s.shape, jnp.bfloat16)
    for i in range(nq):
        if i in resumed:
            m_s[i] = state_in[i][1][...]
            continue
        for head in range(HEADS_DEV):
            s = scores(kv_s[0, :SAMPLE, :], q_head(q_s, i, head))
            top = jnp.max(s, axis=0, keepdims=True) * SCALE
            m_s[i, head] = jnp.broadcast_to(top, (8, QB))
    order_copy.wait()

    def order_at(step):
        return order_ref[x * 8 + lax.rem(z + step, 4) * 2 + core]

    def block_at(step):
        return lax.rem(x + step[0], 4) * 8 + z * 2 + lax.rem(core + step[1], 2)

    def reaches(order, block):
        return block <= FIRST_BLOCK + order // 2

    orders = [order_at(step) for step in z_steps]
    blocks = [block_at(step) for step in kv_steps]
    taken = {}
    if own_early is not None:
        load = jnp.int32(0)
        for z_step in FIRST:
            for step in HERE:
                load += reaches(order_at(z_step), block_at(step)).astype(jnp.int32)
        for step in HERE:
            early = reaches(order_at(0), block_at(step)) & (load < EARLY_PAIRS)
            load += early.astype(jnp.int32)
            taken[step] = early if own_early else jnp.logical_not(early)
    for j, block in enumerate(blocks):
        block_s[j] = block
    count = edges = jnp.int32(0)
    for qi, kj in pairs:
        last = FIRST_BLOCK + orders[qi] // 2
        list_q[count] = qi
        list_k[count] = kj
        mine = taken.get(kv_steps[kj], True) if z_steps[qi] == 0 else True
        count += ((blocks[kj] < last) & mine).astype(jnp.int32)
        for first in (0, QB):
            for column, value in enumerate((qi, kj, orders[qi], blocks[kj], first)):
                edge_s[edges, column] = value
            seen = (blocks[kj] == last) & mine
            if first > 0:
                seen = seen & (lax.rem(orders[qi], 2) == 1)
            edges += seen.astype(jnp.int32)

    def wait_upto(done, needed):
        def wait_one(j, carry):
            for half in range(2):
                kv_copy(j, half).wait()
            return carry

        lax.fori_loop(done, needed + 1, wait_one, 0)
        return jnp.maximum(done, needed + 1)

    parts = range(0, KV_DEV, PART)

    def pair(t, carry):
        q_old, k_old, here = carry
        qi, kj = list_q[t], list_k[t]
        after = jnp.minimum(t + 1, count - 1)
        q_next, k_next = list_q[after], list_k[after]
        here = wait_upto(here, k_next)
        s = [s_s[i : i + PART, :] for i in parts]
        p_old = [p_s[i : i + PART, :] for i in parts]
        for head in range(HEADS_DEV):
            if head + 1 < HEADS_DEV:
                q_then, k_then, head_then = qi, kj, head + 1
            else:
                q_then, k_then, head_then = q_next, k_next, 0
            if head > 0:
                q_old, k_old = qi, kj
            head_old = (head - 1) % HEADS_DEV
            ref_point = m_s[qi, head, :1, :]
            s_next, p_new, total = [], [], acc_s[q_old, head_old]
            for n, i in enumerate(parts):
                s_next.append(
                    scores(kv_s[k_then, i : i + PART, :], q_head(q_s, q_then, head_then))
                )
                p_new.append(probabilities(s[n], ref_point).astype(jnp.bfloat16))
                total = total + values_product(kv_s, k_old, p_old[n], i)
            acc_s[q_old, head_old] = total
            s, p_old = s_next, p_new
        for n, i in enumerate(parts):
            s_s[i : i + PART, :] = s[n]
            p_s[i : i + PART, :] = p_old[n]
        return qi, kj, here

    here = wait_upto(jnp.int32(1), list_k[0])
    s_s[...] = scores(keys_of(kv_s, list_k[0]), q_head(q_s, list_q[0], 0))
    q_last, k_last, here = lax.fori_loop(0, count, pair, (list_q[0], list_k[0], here))
    wait_upto(here, jnp.int32(now - 1))

    def edge(t, carry):
        qi, kj, order, block = [edge_s[t, column] for column in range(4)]
        first = pl.multiple_of(edge_s[t, 4], QB)
        masked_step(q_s, kv_s, m_s, acc_s, qi, kj, order, block, first)
        return carry

    lax.fori_loop(0, edges, edge, 0)
    q_last = 0 if nq == 1 else q_last
    acc_s[q_last, HEADS_DEV - 1] += values_product(kv_s, k_last, p_s[...])
    if not final:
        for i in range(nq):
            state_out[i][0][...] = acc_s[i]
            state_out[i][1][...] = m_s[i]
        return
    for i in resumed:
        acc_s[i] += state_in[i][0][...]

    row = lax.broadcasted_iota(jnp.int32, (STATS, QB), 0)

    def finish(i):
        logs = jnp.zeros((STATS, QB), jnp.float32)
        for head in range(HEADS_DEV):
            total = acc_s[i, head, HD : HD + 1, :]
            outs[i][head * HD : (head + 1) * HD, :] = (
                acc_s[i, head, :HD, :] * (1.0 / total)
            ).astype(jnp.bfloat16)
            rest = m_s[i, head, :1, :] + jnp.log2(total)
            for piece in range(3):
                part = rest.astype(jnp.bfloat16).astype(jnp.float32)
                logs = jnp.where(row == stat_row(head, piece), part, logs)
                rest = rest - part
        outs[i][HEADS_DEV * HD :, :] = logs.astype(jnp.bfloat16)

    def redo(qi, order):
        m_s[qi] = jnp.full(m_s.shape[1:], LOW, jnp.float32)
        acc_s[qi] = jnp.zeros(acc_s.shape[1:], jnp.float32)

        def step(t, carry):
            kj = t // (KV_DEV // PART)
            first = pl.multiple_of(lax.rem(t, KV_DEV // PART) * PART, PART)
            block = block_s[kj]

            @pl.when(block <= FIRST_BLOCK + order // 2)
            def _():
                running_step(q_s, kv_s, m_s, acc_s, qi, kj, order, block, first)

            return carry

        lax.fori_loop(0, nkv * (KV_DEV // PART), step, 0)

    for i in range(nq):
        finish(i)
    totals = acc_s[:, :, HD : HD + 8, :]
    bad = jnp.max(jnp.where((totals > 1.0 / SAFE) & (totals < SAFE), 0.0, 1.0))

    @pl.when(bad > 0.0)
    def _():
        for copy in kv_copies[2 * now :]:
            copy.start()
        for copy in kv_copies[2 * now :]:
            copy.wait()
        for i in range(nq):
            redo(i, orders[i])
            finish(i)


def attend(
    block_order,
    queries,
    z_steps,
    blocks,
    kv_steps,
    pairs,
    states=None,
    final=True,
    own_early=None,
):
    states = states or {}
    nq, nkv = len(queries), len(kv_steps)
    any_spec = pl.BlockSpec(memory_space=pl.ANY)
    vmem_spec = pl.BlockSpec(memory_space=pltpu.VMEM)
    acc_shape, m_shape = (HEADS_DEV, HD + SUMS, QB), (HEADS_DEV, 8, QB)
    if final:
        outs = [jax.ShapeDtypeStruct((HEADS_DEV * HD + STATS, QB), jnp.bfloat16)] * nq
    else:
        outs = [jax.ShapeDtypeStruct(shape, jnp.float32) for shape in (acc_shape, m_shape)] * nq
    results = pl.pallas_call(
        lambda *refs: attend_kernel(
            z_steps, kv_steps, pairs, sorted(states), final, own_early, *refs
        ),
        out_shape=outs,
        in_specs=[any_spec]
        + [vmem_spec] * (nq + 1)
        + [any_spec] * (nkv - 1)
        + [vmem_spec] * (2 * len(states)),
        out_specs=[vmem_spec] * len(outs),
        scratch_shapes=[
            pltpu.VMEM((nq, *acc_shape), jnp.float32),
            pltpu.VMEM((nq, *m_shape), jnp.float32),
            pltpu.VMEM((nq, QB, HEADS_DEV * HD), jnp.bfloat16),
            pltpu.VMEM((nkv, 2 * KV_DEV, HD), jnp.bfloat16),
            pltpu.VMEM((KV_DEV, QB), jnp.float32),
            pltpu.VMEM((KV_DEV, QB), jnp.bfloat16),
            pltpu.SMEM(block_order.shape, jnp.int32),
            pltpu.SMEM((len(pairs) + 1,), jnp.int32),
            pltpu.SMEM((len(pairs) + 1,), jnp.int32),
            pltpu.SMEM((2 * len(pairs) + 1, 5), jnp.int32),
            pltpu.SMEM((nkv,), jnp.int32),
            pltpu.SemaphoreType.DMA,
            pltpu.SemaphoreType.DMA((nkv, 2)),
        ],
        compiler_params=pltpu.CompilerParams(vmem_limit_bytes=28 * 1024 * 1024),
        cost_estimate=pl.CostEstimate(
            flops=4 * len(pairs) * QROWS * KV_DEV * HD,
            bytes_accessed=nq * QROWS * HD * 4 + nkv * KV_DEV * HD * 4,
            transcendentals=len(pairs) * QROWS * KV_DEV,
        ),
        name="attend",
    )(
        block_order,
        *queries,
        *[blocks[step] for step in kv_steps],
        *[array for i in sorted(states) for array in states[i]],
    )
    return results if final else [tuple(results[2 * i : 2 * i + 2]) for i in range(nq)]


def pack(keys, values):
    pieces = values.reshape(KV_DEV // HD, HD, HD).swapaxes(1, 2).reshape(KV_DEV, HD)
    return jnp.concatenate([keys, pieces], axis=0)


def combine_kernel(*refs):
    parts, result = refs[:NZ], refs[NZ]
    stats = [part[HEADS_DEV * HD :, :].astype(jnp.float32) for part in parts]
    for head in range(HEADS_DEV):
        rows = [stat_row(head, piece) for piece in range(3)]
        logs = [sum(stat[r : r + 1, :] for r in rows) for stat in stats]
        top = logs[0]
        for log in logs[1:]:
            top = jnp.maximum(top, log)
        weights = [jnp.exp2(log - top) for log in logs]
        share = 1.0 / sum(weights)
        columns = slice(head * HD, (head + 1) * HD)
        gathered = jnp.zeros((HD, QB), jnp.float32)
        for weight, part in zip(weights, parts):
            gathered = gathered + weight * share * part[columns, :].astype(jnp.float32)
        result[:, columns] = gathered.T.astype(jnp.bfloat16)


def combine(parts):
    vmem_spec = pl.BlockSpec(memory_space=pltpu.VMEM)
    return pl.pallas_call(
        combine_kernel,
        out_shape=jax.ShapeDtypeStruct((QB, HEADS_DEV * HD), jnp.bfloat16),
        in_specs=[vmem_spec] * NZ,
        out_specs=vmem_spec,
        compiler_params=pltpu.CompilerParams(vmem_limit_bytes=32 * 1024 * 1024),
        cost_estimate=pl.CostEstimate(
            flops=8 * NZ * QROWS * HD,
            bytes_accessed=(NZ + 1) * QROWS * HD * 2,
            transcendentals=NZ * QROWS,
        ),
        name="combine",
    )(*parts)


def every(queries, keys):
    return tuple((qi, kj) for qi in queries for kj in keys)


def body(queries, keys, values, block_order):
    def key_block(step):
        return lax.ppermute(own, "x", ring(4, -step))

    def query_block(value, step):
        return lax.ppermute(value, "z", ring(4, -step))

    def give_back(part, step):
        return lax.ppermute(part, "z", ring(4, step))

    own = pack(keys, values)
    blocks = {(0, 0): own, (1, 0): key_block(1), (3, 0): key_block(3), (0, 1): swap_core(own)}
    back, ahead = query_block(queries, 3), query_block(queries, 1)
    far, back, ahead = lax.optimization_barrier((queries, back, ahead))
    far = query_block(far, 2)
    near = blocks[1, 0], blocks[3, 0]
    own, back, ahead, near = lax.optimization_barrier((own, back, ahead, near))
    blocks[1, 0], blocks[3, 0] = near
    blocks[2, 0] = key_block(2)
    for step in (1, 3):
        blocks[step, 1] = swap_core(blocks[step, 0])
    *states, own_state = attend(
        block_order,
        [back, ahead, queries],
        FIRST + (0,),
        blocks,
        HERE,
        every((0, 1, 2), range(4)),
        final=False,
        own_early=True,
    )
    states, far, blocks[2, 0] = lax.optimization_barrier((states, far, blocks[2, 0]))
    blocks[2, 1] = swap_core(blocks[2, 0])
    to_back, to_ahead = attend(
        block_order,
        [back, ahead],
        FIRST,
        blocks,
        LATER + HERE,
        every((0, 1), range(4)),
        dict(enumerate(states)),
    )
    to_back, to_ahead, far = lax.optimization_barrier((to_back, to_ahead, far))
    here = [give_back(to_back, 3), give_back(to_ahead, 1)]
    (to_far,) = attend(block_order, [far], (2,), blocks, HERE + LATER, every((0,), range(8)))
    to_far, queries, here = lax.optimization_barrier((to_far, queries, here))
    here.append(give_back(to_far, 2))
    (own_part,) = attend(
        block_order,
        [queries],
        (0,),
        blocks,
        LATER + HERE,
        every((0,), range(8)),
        {0: own_state},
        own_early=False,
    )
    return combine([own_part, *here])


def solution(mesh):
    split = Mesh(mesh.devices.reshape(4, 4, 2, 4), ("x", "z", "core", "qh"))
    ctx = ("x", "z", "core")
    in_specs = (P(ctx, "qh"), P(ctx, None), P(ctx, None), P())
    out_specs = P(ctx, "qh")
    return jax.shard_map(body, mesh=split, in_specs=in_specs, out_specs=out_specs, check_vma=False)
```

```python
import math

import jax
import jax.numpy as jnp
from jax import lax
from jax.experimental import pallas as pl
from jax.experimental.pallas import tpu as pltpu
from jax.sharding import Mesh, PartitionSpec as P

HD = 128
KV_DEV = 1024
QB = 512
HEADS_DEV = 2
QROWS = QB * HEADS_DEV
SUMS = 16
SAMPLE = 128
PART = 512
FIRST_BLOCK = 16
SCALE = 1.4426950408889634 / math.sqrt(HD)
LOW = -1e30
SAFE = 2.0**100
NZ = 4
HERE = ((0, 0), (0, 1), (1, 0), (3, 0))
LATER = ((1, 1), (3, 1), (2, 0), (2, 1))
FIRST = (3, 1)
EARLY_PAIRS = 10
STATS = 16
NT = (((1,), (1,)), ((), ()))


def ring(size, step):
    return [(i, (i + step) % size) for i in range(size)]


def swap_core(value):
    return lax.ppermute(value, "core", [(0, 1), (1, 0)])


def scores(keys, q):
    return lax.dot_general(keys, q, NT, preferred_element_type=jnp.float32)


def visible_keys(order, block, first, count):
    k_pos = block * KV_DEV + first + lax.broadcasted_iota(jnp.int32, (count, QB), 0)
    q_pos = FIRST_BLOCK * KV_DEV + order * QB + lax.broadcasted_iota(jnp.int32, (count, QB), 1)
    return k_pos <= q_pos


def q_head(q_s, qi, head):
    return q_s[qi, :, head * HD : (head + 1) * HD]


def keys_of(kv_s, kj):
    return kv_s[kj, :KV_DEV, :]


def values_product(kv_s, kj, p, first=0):
    count = p.shape[0]
    starts = [KV_DEV + first + i for i in range(0, count, HD)]
    across = jnp.concatenate([kv_s[kj, pl.ds(i, HD), :] for i in starts], axis=1)
    tall = jnp.concatenate([across, jnp.ones((SUMS, count), jnp.bfloat16)], axis=0)
    return jnp.dot(tall, p, preferred_element_type=jnp.float32)


def stat_row(head, piece):
    return head * 3 + piece


def probabilities(s, ref_point):
    return jnp.exp2(s * SCALE - ref_point)


def masked_step(q_s, kv_s, m_s, acc_s, qi, kj, order, block, first):
    visible = visible_keys(order, block, first, QB)
    for head in range(HEADS_DEV):
        s = scores(kv_s[kj, pl.ds(first, QB), :], q_head(q_s, qi, head))
        p = probabilities(s, m_s[qi, head, :1, :])
        p = jnp.where(visible, p, 0.0).astype(jnp.bfloat16)
        acc_s[qi, head] += values_product(kv_s, kj, p, first)


def running_step(q_s, kv_s, m_s, acc_s, qi, kj, order, block, first):
    visible = visible_keys(order, block, first, PART)
    for head in range(HEADS_DEV):
        s = scores(kv_s[kj, pl.ds(first, PART), :], q_head(q_s, qi, head))
        s = jnp.where(visible, s * SCALE, LOW)
        m_old = m_s[qi, head]
        m_new = jnp.maximum(m_old, jnp.max(s, axis=0, keepdims=True))
        p = jnp.where(visible, jnp.exp2(s - m_new[:1]), 0.0).astype(jnp.bfloat16)
        m_s[qi, head] = m_new
        acc_s[qi, head] = acc_s[qi, head] * jnp.exp2(m_old - m_new)[:1] + values_product(
            kv_s, kj, p, first
        )


def attend_kernel(z_steps, kv_steps, pairs, resumed, final, own_early, order_in, *refs):
    nq, nkv = len(z_steps), len(kv_steps)
    now = 1 + max(kj for _, kj in pairs)
    refs = list(refs)
    q_in = [refs.pop(0) for _ in range(nq)]
    kv_in = [refs.pop(0) for _ in range(nkv)]
    state_in = {i: (refs.pop(0), refs.pop(0)) for i in resumed}
    if final:
        outs = [refs.pop(0) for _ in range(nq)]
    else:
        state_out = [(refs.pop(0), refs.pop(0)) for _ in range(nq)]
    acc_s, m_s, q_s, kv_s, s_s, p_s, order_ref, list_q, list_k, edge_s, block_s = refs[:11]
    order_sem, kv_sem = refs[11:]
    x = lax.axis_index("x")
    z = lax.axis_index("z")
    core = lax.axis_index("core")

    def kv_copy(j, half, source=1):
        rows = pl.ds(half * KV_DEV, KV_DEV)
        return pltpu.make_async_copy(
            kv_in[source].at[rows, :], kv_s.at[j, rows, :], kv_sem.at[j, half]
        )

    order_copy = pltpu.make_async_copy(order_in, order_ref, order_sem)
    kv_copies = [kv_copy(j, half, j) for j in range(nkv) for half in range(2)]
    for copy in [order_copy, *kv_copies[2 : 2 * now]]:
        copy.start()
    for i in range(nq):
        q_s[i] = q_in[i][...]
    kv_s[0] = kv_in[0][...]
    acc_s[...] = jnp.zeros(acc_s.shape, jnp.float32)
    p_s[...] = jnp.zeros(p_s.shape, jnp.bfloat16)
    for i in range(nq):
        if i in resumed:
            m_s[i] = state_in[i][1][...]
            continue
        for head in range(HEADS_DEV):
            s = scores(kv_s[0, :SAMPLE, :], q_head(q_s, i, head))
            top = jnp.max(s, axis=0, keepdims=True) * SCALE
            m_s[i, head] = jnp.broadcast_to(top, (8, QB))
    order_copy.wait()

    def order_at(step):
        return order_ref[x * 8 + lax.rem(z + step, 4) * 2 + core]

    def block_at(step):
        return lax.rem(x + step[0], 4) * 8 + z * 2 + lax.rem(core + step[1], 2)

    def reaches(order, block):
        return block <= FIRST_BLOCK + order // 2

    orders = [order_at(step) for step in z_steps]
    blocks = [block_at(step) for step in kv_steps]
    taken = {}
    if own_early is not None:
        load = jnp.int32(0)
        for z_step in FIRST:
            for step in HERE:
                load += reaches(order_at(z_step), block_at(step)).astype(jnp.int32)
        for step in HERE:
            early = reaches(order_at(0), block_at(step)) & (load < EARLY_PAIRS)
            load += early.astype(jnp.int32)
            taken[step] = early if own_early else jnp.logical_not(early)
    for j, block in enumerate(blocks):
        block_s[j] = block
    count = edges = jnp.int32(0)
    for qi, kj in pairs:
        last = FIRST_BLOCK + orders[qi] // 2
        list_q[count] = qi
        list_k[count] = kj
        mine = taken.get(kv_steps[kj], True) if z_steps[qi] == 0 else True
        count += ((blocks[kj] < last) & mine).astype(jnp.int32)
        for first in (0, QB):
            for column, value in enumerate((qi, kj, orders[qi], blocks[kj], first)):
                edge_s[edges, column] = value
            seen = (blocks[kj] == last) & mine
            if first > 0:
                seen = seen & (lax.rem(orders[qi], 2) == 1)
            edges += seen.astype(jnp.int32)

    def wait_upto(done, needed):
        def wait_one(j, carry):
            for half in range(2):
                kv_copy(j, half).wait()
            return carry

        lax.fori_loop(done, needed + 1, wait_one, 0)
        return jnp.maximum(done, needed + 1)

    parts = range(0, KV_DEV, PART)

    def pair(t, carry):
        q_old, k_old, here = carry
        qi, kj = list_q[t], list_k[t]
        after = jnp.minimum(t + 1, count - 1)
        q_next, k_next = list_q[after], list_k[after]
        if nq == 1:
            q_old = qi = q_next = 0
        here = wait_upto(here, k_next)
        s = [s_s[i : i + PART, :] for i in parts]
        p_old = [p_s[i : i + PART, :] for i in parts]
        for head in range(HEADS_DEV):
            if head + 1 < HEADS_DEV:
                q_then, k_then, head_then = qi, kj, head + 1
            else:
                q_then, k_then, head_then = q_next, k_next, 0
            if head > 0:
                q_old, k_old = qi, kj
            head_old = (head - 1) % HEADS_DEV
            ref_point = m_s[qi, head, :1, :]
            s_next, p_new, total = [], [], acc_s[q_old, head_old]
            for n, i in enumerate(parts):
                s_next.append(
                    scores(kv_s[k_then, i : i + PART, :], q_head(q_s, q_then, head_then))
                )
                p_new.append(probabilities(s[n], ref_point).astype(jnp.bfloat16))
                total = total + values_product(kv_s, k_old, p_old[n], i)
            acc_s[q_old, head_old] = total
            s, p_old = s_next, p_new
        for n, i in enumerate(parts):
            s_s[i : i + PART, :] = s[n]
            p_s[i : i + PART, :] = p_old[n]
        return jnp.int32(qi), kj, here

    here = wait_upto(jnp.int32(1), list_k[0])
    s_s[...] = scores(keys_of(kv_s, list_k[0]), q_head(q_s, list_q[0], 0))
    q_last, k_last, here = lax.fori_loop(0, count, pair, (list_q[0], list_k[0], here))
    wait_upto(here, jnp.int32(now - 1))

    def edge(t, carry):
        qi, kj, order, block = [edge_s[t, column] for column in range(4)]
        first = pl.multiple_of(edge_s[t, 4], QB)
        masked_step(q_s, kv_s, m_s, acc_s, qi, kj, order, block, first)
        return carry

    lax.fori_loop(0, edges, edge, 0)
    q_last = 0 if nq == 1 else q_last
    acc_s[q_last, HEADS_DEV - 1] += values_product(kv_s, k_last, p_s[...])
    if not final:
        for i in range(nq):
            state_out[i][0][...] = acc_s[i]
            state_out[i][1][...] = m_s[i]
        return
    for i in resumed:
        acc_s[i] += state_in[i][0][...]

    row = lax.broadcasted_iota(jnp.int32, (STATS, QB), 0)

    def finish(i):
        logs = jnp.zeros((STATS, QB), jnp.float32)
        for head in range(HEADS_DEV):
            total = acc_s[i, head, HD : HD + 1, :]
            outs[i][head * HD : (head + 1) * HD, :] = (
                acc_s[i, head, :HD, :] * (1.0 / total)
            ).astype(jnp.bfloat16)
            rest = m_s[i, head, :1, :] + jnp.log2(total)
            for piece in range(3):
                part = rest.astype(jnp.bfloat16).astype(jnp.float32)
                logs = jnp.where(row == stat_row(head, piece), part, logs)
                rest = rest - part
        outs[i][HEADS_DEV * HD :, :] = logs.astype(jnp.bfloat16)

    def redo(qi, order):
        m_s[qi] = jnp.full(m_s.shape[1:], LOW, jnp.float32)
        acc_s[qi] = jnp.zeros(acc_s.shape[1:], jnp.float32)

        def step(t, carry):
            kj = t // (KV_DEV // PART)
            first = pl.multiple_of(lax.rem(t, KV_DEV // PART) * PART, PART)
            block = block_s[kj]

            @pl.when(block <= FIRST_BLOCK + order // 2)
            def _():
                running_step(q_s, kv_s, m_s, acc_s, qi, kj, order, block, first)

            return carry

        lax.fori_loop(0, nkv * (KV_DEV // PART), step, 0)

    for i in range(nq):
        finish(i)
    totals = acc_s[:, :, HD : HD + 8, :]
    bad = jnp.max(jnp.where((totals > 1.0 / SAFE) & (totals < SAFE), 0.0, 1.0))

    @pl.when(bad > 0.0)
    def _():
        for copy in kv_copies[2 * now :]:
            copy.start()
        for copy in kv_copies[2 * now :]:
            copy.wait()
        for i in range(nq):
            redo(i, orders[i])
            finish(i)


def attend(
    block_order,
    queries,
    z_steps,
    blocks,
    kv_steps,
    pairs,
    states=None,
    final=True,
    own_early=None,
):
    states = states or {}
    nq, nkv = len(queries), len(kv_steps)
    any_spec = pl.BlockSpec(memory_space=pl.ANY)
    vmem_spec = pl.BlockSpec(memory_space=pltpu.VMEM)
    acc_shape, m_shape = (HEADS_DEV, HD + SUMS, QB), (HEADS_DEV, 8, QB)
    if final:
        outs = [jax.ShapeDtypeStruct((HEADS_DEV * HD + STATS, QB), jnp.bfloat16)] * nq
    else:
        outs = [jax.ShapeDtypeStruct(shape, jnp.float32) for shape in (acc_shape, m_shape)] * nq
    results = pl.pallas_call(
        lambda *refs: attend_kernel(
            z_steps, kv_steps, pairs, sorted(states), final, own_early, *refs
        ),
        out_shape=outs,
        in_specs=[any_spec]
        + [vmem_spec] * (nq + 1)
        + [any_spec] * (nkv - 1)
        + [vmem_spec] * (2 * len(states)),
        out_specs=[vmem_spec] * len(outs),
        scratch_shapes=[
            pltpu.VMEM((nq, *acc_shape), jnp.float32),
            pltpu.VMEM((nq, *m_shape), jnp.float32),
            pltpu.VMEM((nq, QB, HEADS_DEV * HD), jnp.bfloat16),
            pltpu.VMEM((nkv, 2 * KV_DEV, HD), jnp.bfloat16),
            pltpu.VMEM((KV_DEV, QB), jnp.float32),
            pltpu.VMEM((KV_DEV, QB), jnp.bfloat16),
            pltpu.SMEM(block_order.shape, jnp.int32),
            pltpu.SMEM((len(pairs) + 1,), jnp.int32),
            pltpu.SMEM((len(pairs) + 1,), jnp.int32),
            pltpu.SMEM((2 * len(pairs) + 1, 5), jnp.int32),
            pltpu.SMEM((nkv,), jnp.int32),
            pltpu.SemaphoreType.DMA,
            pltpu.SemaphoreType.DMA((nkv, 2)),
        ],
        compiler_params=pltpu.CompilerParams(vmem_limit_bytes=28 * 1024 * 1024),
        cost_estimate=pl.CostEstimate(
            flops=4 * len(pairs) * QROWS * KV_DEV * HD,
            bytes_accessed=nq * QROWS * HD * 4 + nkv * KV_DEV * HD * 4,
            transcendentals=len(pairs) * QROWS * KV_DEV,
        ),
        name="attend",
    )(
        block_order,
        *queries,
        *[blocks[step] for step in kv_steps],
        *[array for i in sorted(states) for array in states[i]],
    )
    return results if final else [tuple(results[2 * i : 2 * i + 2]) for i in range(nq)]


def pack(keys, values):
    pieces = values.reshape(KV_DEV // HD, HD, HD).swapaxes(1, 2).reshape(KV_DEV, HD)
    return jnp.concatenate([keys, pieces], axis=0)


def combine_kernel(*refs):
    parts, result = refs[:NZ], refs[NZ]
    stats = [part[HEADS_DEV * HD :, :].astype(jnp.float32) for part in parts]
    for head in range(HEADS_DEV):
        rows = [stat_row(head, piece) for piece in range(3)]
        logs = [sum(stat[r : r + 1, :] for r in rows) for stat in stats]
        top = logs[0]
        for log in logs[1:]:
            top = jnp.maximum(top, log)
        weights = [jnp.exp2(log - top) for log in logs]
        share = 1.0 / sum(weights)
        columns = slice(head * HD, (head + 1) * HD)
        gathered = jnp.zeros((HD, QB), jnp.float32)
        for weight, part in zip(weights, parts):
            gathered = gathered + weight * share * part[columns, :].astype(jnp.float32)
        result[:, columns] = gathered.T.astype(jnp.bfloat16)


def combine(parts):
    vmem_spec = pl.BlockSpec(memory_space=pltpu.VMEM)
    return pl.pallas_call(
        combine_kernel,
        out_shape=jax.ShapeDtypeStruct((QB, HEADS_DEV * HD), jnp.bfloat16),
        in_specs=[vmem_spec] * NZ,
        out_specs=vmem_spec,
        compiler_params=pltpu.CompilerParams(vmem_limit_bytes=32 * 1024 * 1024),
        cost_estimate=pl.CostEstimate(
            flops=8 * NZ * QROWS * HD,
            bytes_accessed=(NZ + 1) * QROWS * HD * 2,
            transcendentals=NZ * QROWS,
        ),
        name="combine",
    )(*parts)


def every(queries, keys):
    return tuple((qi, kj) for qi in queries for kj in keys)


def body(queries, keys, values, block_order):
    def key_block(step):
        return lax.ppermute(own, "x", ring(4, -step))

    def query_block(value, step):
        return lax.ppermute(value, "z", ring(4, -step))

    def give_back(part, step):
        return lax.ppermute(part, "z", ring(4, step))

    own = pack(keys, values)
    blocks = {(0, 0): own, (1, 0): key_block(1), (3, 0): key_block(3), (0, 1): swap_core(own)}
    back, ahead = query_block(queries, 3), query_block(queries, 1)
    far, back, ahead = lax.optimization_barrier((queries, back, ahead))
    far = query_block(far, 2)
    near = blocks[1, 0], blocks[3, 0]
    own, back, ahead, near = lax.optimization_barrier((own, back, ahead, near))
    blocks[1, 0], blocks[3, 0] = near
    blocks[2, 0] = key_block(2)
    for step in (1, 3):
        blocks[step, 1] = swap_core(blocks[step, 0])
    *states, own_state = attend(
        block_order,
        [back, ahead, queries],
        FIRST + (0,),
        blocks,
        HERE,
        every((0, 1, 2), range(4)),
        final=False,
        own_early=True,
    )
    states, far, blocks[2, 0] = lax.optimization_barrier((states, far, blocks[2, 0]))
    blocks[2, 1] = swap_core(blocks[2, 0])
    to_back, to_ahead = attend(
        block_order,
        [back, ahead],
        FIRST,
        blocks,
        LATER + HERE,
        every((0, 1), range(4)),
        dict(enumerate(states)),
    )
    to_back, to_ahead, far = lax.optimization_barrier((to_back, to_ahead, far))
    here = [give_back(to_back, 3), give_back(to_ahead, 1)]
    (to_far,) = attend(block_order, [far], (2,), blocks, HERE + LATER, every((0,), range(8)))
    to_far, queries, here = lax.optimization_barrier((to_far, queries, here))
    here.append(give_back(to_far, 2))
    (own_part,) = attend(
        block_order,
        [queries],
        (0,),
        blocks,
        LATER + HERE,
        every((0,), range(8)),
        {0: own_state},
        own_early=False,
    )
    return combine([own_part, *here])


def solution(mesh):
    split = Mesh(mesh.devices.reshape(4, 4, 2, 4), ("x", "z", "core", "qh"))
    ctx = ("x", "z", "core")
    in_specs = (P(ctx, "qh"), P(ctx, None), P(ctx, None), P())
    out_specs = P(ctx, "qh")
    return jax.shard_map(body, mesh=split, in_specs=in_specs, out_specs=out_specs, check_vma=False)
```
